32 devices in a mesh: pair: 8 (over z, y), virt: 4 (over x, core).
Axes of the slice: x: 2, y: 2, z: 4, core: 2. Of those that a mesh axis runs over, the one named last changes fastest.
Arguments:
- amplitudes: bfloat16 [2, 112, 960, 960], P(None, 'pair', None, 'virt'), may hold values from -6 to 6
- integrals: bfloat16 [112, 960, 2, 960], P('pair', 'virt'), may hold values from -0.02734375 to 0.02734375
Outputs:
- residual_tile: float32 [2, 960, 2, 960], P(None, 'pair', None, 'virt')
The draws below stay inside these ranges and needn't reach their ends.
All inputs are finite; a program needn't handle non-finite values.
Results may differ from the reference program's by a relative error of at most 0.0003.
Values may be sent and summed in bfloat16 or wider, within the bound.
No kernel may reach another device: no remote copies, remote signals or barrier semaphores. Data moves between devices by JAX's collectives and lax.ppermute only.
A program may use at most 320 MiB of HBM per device.

```python
import jax
import jax.numpy as jnp
from jax import lax

O = 112
V = 960
NB = 2


def raised(drawn, rng, source, target, parts, factor):
    owner, partner = [(jnp.arange(drawn.shape[axis_at]) // (drawn.shape[axis_at] // parts)).reshape([-1 if axis == axis_at else 1 for axis in range(drawn.ndim)]) for axis_at in (source, target)]
    chosen = jax.random.permutation(rng, parts)[partner]
    strong = (owner == chosen) | (owner == (partner + parts // 2) % parts)
    return jnp.where(strong, factor * drawn, drawn)


def shard_levels(key, dims, split, least, largest):
    factor_of = 1.0
    for axis_at, blocks in split:
        steps = jax.random.uniform(jax.random.fold_in(jax.random.fold_in(key, 6), axis_at), (blocks,), jnp.float32, least / len(split), largest / len(split))
        factor_of = factor_of * jnp.repeat(jnp.exp(steps), dims[axis_at] // blocks).reshape((-1,) + (1,) * (len(dims) - 1 - axis_at))
    return factor_of


def noise(stream_key, shape, width, bound, cuts=(), held_as=jnp.bfloat16):
    gain = shard_levels(stream_key, shape, cuts, -0.22, 0.18) if cuts else 1.0
    entries = jax.random.normal(stream_key, shape, jnp.float32) * width * gain
    return jnp.minimum(jnp.maximum(entries, -bound), bound).astype(held_as)


def heavy_noise(key, extent, width, most, shards, heavy, held_as=jnp.bfloat16):
    entries = width * jax.random.normal(key, extent, jnp.float32)
    if shards:
        entries = entries * shard_levels(key, extent, shards, -0.22, 0.18)
    return jnp.clip(raised(entries, jax.random.fold_in(key, 3), *heavy), -most, most).astype(held_as)


def setup_inputs(seed: int = 0) -> dict:
    key_list = jax.random.split(jax.random.key(seed), 3)
    amplitudes = noise(key_list[0], (NB, O, V, V), 1.0, 6.0, ((1, 8), (3, 4)))
    integrals = heavy_noise(key_list[1], (O, V, NB, V), (O * V) ** -0.5, 0.02734375, ((0, 8), (1, 4)), (1, 3, 4, 2.0))
    return dict(amplitudes=amplitudes, integrals=integrals)


def reference(amplitudes, integrals):
    def accumulate(running, index):
        upper = lax.dynamic_index_in_dim(amplitudes, index, 1, keepdims=False).astype(jnp.float32)
        lower = lax.dynamic_index_in_dim(integrals, index, 0, keepdims=False).astype(jnp.float32)
        return running + jnp.einsum("iac,cjb->iajb", upper, lower), None

    initial = jnp.zeros((NB, V, NB, V), jnp.float32)
    cycle, unused = lax.scan(accumulate, initial, jnp.arange(O, dtype=jnp.int32))
    return cycle + cycle.transpose(2, 3, 0, 1)
```

```python
import jax
import jax.numpy as jnp
from jax import lax
from jax.sharding import PartitionSpec as P

AXES = ("pair", "virt")
TOP = 12


def products(amplitudes, integrals):
    return [
        [
            jnp.einsum("kac,kcb->ab", amplitudes[i], integrals[:, :, j], preferred_element_type=jnp.float32)
            for j in range(2)
        ]
        for i in range(2)
    ]


def with_extras(block, diagonal, nv, width):
    rows, cols = block.shape
    largest = jnp.maximum(jnp.max(jnp.abs(block)), jnp.max(jnp.abs(diagonal)))
    parts = block.reshape(rows, nv, cols // nv).transpose(1, 0, 2)
    extra = jnp.stack([diagonal, jnp.full((rows,), largest)], axis=1)
    extra = jnp.pad(extra, ((0, 0), (0, width - cols // nv - 2)))
    return jnp.concatenate([parts, jnp.broadcast_to(extra, (nv, *extra.shape))], axis=2)


def coded(values, bound, at):
    exponent = jnp.clip(jnp.floor(jnp.log2(jnp.maximum(bound, 1e-30))), -100.0, 100.0)
    column = lax.broadcasted_iota(jnp.int32, values.shape, values.ndim - 1)
    return jnp.where(column == at, exponent, values * jnp.exp2(TOP - exponent)).astype(jnp.float16)


def decoded(block, at):
    exponent = block[..., at : at + 1].astype(jnp.float32)
    values = block.astype(jnp.float32) * jnp.exp2(exponent - TOP)
    column = lax.broadcasted_iota(jnp.int32, values.shape, values.ndim - 1)
    return jnp.where(column == at, jnp.exp2(exponent + 1.0), values)


def solution(mesh):
    np_, nv = mesh.shape["pair"], mesh.shape["virt"]
    nx, nz, ratio = nv // 2, np_ // 2, np_ // nv

    def permutation(move):
        pairs = []
        for p in range(np_):
            for v in range(nv):
                q, w = move(p, v)
                pairs.append((p * nv + v, q * nv + w))
        return pairs

    swap_core = permutation(lambda p, v: (p, v ^ 1))

    def send(block, pairs):
        return lax.ppermute(block, AXES, pairs)

    def reduced(chunk, at):
        p, v = lax.axis_index("pair"), lax.axis_index("virt")
        x, core, z, y = v // 2, v % 2, p // 2, p % 2
        width = chunk.shape[-1]
        chunk = chunk.reshape(nx, 2, nz, 2, -1, width)
        kept = lax.dynamic_index_in_dim(chunk, core, 1, keepdims=False)
        other = lax.dynamic_index_in_dim(chunk, 1 - core, 1, keepdims=False)
        chip = kept + send(other, swap_core)

        def pick(array, x_at, y_at):
            array = lax.dynamic_index_in_dim(array, x_at, 0, keepdims=False)
            return lax.dynamic_index_in_dim(array, y_at, 1, keepdims=False)

        plane = pick(chip, x, y)
        arrived = []
        for dx in range(nx):
            for dy in range(2):
                if dx or dy:
                    block = pick(chip, (x + dx) % nx, (y + dy) % 2)
                    block = coded(block, block[..., at : at + 1], at)
                    pairs = permutation(lambda p, v: (p ^ dy, (v + 2 * dx) % nv))
                    arrived.append(send(block, pairs))
        for block in arrived:
            plane = plane + decoded(block, at)
        total = lax.dynamic_index_in_dim(plane, z, 0, keepdims=False)
        arrived = []
        for dz in range(1, nz):
            block = lax.dynamic_index_in_dim(plane, (z + dz) % nz, 0, keepdims=False)
            block = coded(block, block[..., at : at + 1], at)
            pairs = permutation(lambda p, v: ((p + 2 * dz) % np_, v))
            arrived.append(send(block, pairs))
        for block in arrived:
            total = total + decoded(block, at)
        return total

    def shards(amplitudes, integrals):
        virtuals = amplitudes.shape[2]
        rows, cols = virtuals // np_, virtuals // nv
        width = -(-(cols + 2) // 128) * 128
        p, v = lax.axis_index("pair"), lax.axis_index("virt")
        (p00, p01), (p10, p11) = products(amplitudes, integrals)
        s01 = p01 + p10.T
        s00, s11 = p00 + p00.T, p11 + p11.T
        a, b = (lax.broadcasted_iota(jnp.int32, (virtuals, virtuals), d) for d in range(2))
        both = jnp.where(a <= b, s00, s11)
        crossed = reduced(with_extras(s01, jnp.zeros((virtuals,)), nv, width), cols + 1)
        same = reduced(with_extras(both, jnp.diagonal(s11), nv, width), cols + 1)

        mine = jnp.stack([crossed[:, :cols], same[:, :cols]])
        tiles = mine.reshape(2, rows, ratio, rows)
        mirrored = jnp.zeros((ratio, 2, rows, rows), jnp.float32)
        for t in range(ratio):
            h = (p % ratio + t) % ratio
            tile = lax.dynamic_index_in_dim(tiles, h, 2, keepdims=False).transpose(0, 2, 1)
            pairs = permutation(lambda p, v: (ratio * v + (p % ratio + t) % ratio, p // ratio))
            from_h = (p - t) % ratio
            mirrored = lax.dynamic_update_index_in_dim(mirrored, send(tile, pairs), from_h, 0)
        mirrored = mirrored.transpose(1, 2, 0, 3).reshape(2, rows, cols)
        a = p * rows + lax.broadcasted_iota(jnp.int32, (rows, cols), 0)
        b = v * cols + lax.broadcasted_iota(jnp.int32, (rows, cols), 1)
        out00 = jnp.where(a <= b, mine[1], mirrored[1])
        out11 = jnp.where(a > b, mine[1], mirrored[1])
        out11 = jnp.where(a == b, same[:, cols : cols + 1], out11)
        return jnp.stack([jnp.stack([out00, mine[0]], 1), jnp.stack([mirrored[0], out11], 1)])

    placed = (P(None, "pair", None, "virt"), P("pair", "virt", None, None))
    return jax.shard_map(
        shards, mesh=mesh, in_specs=placed, out_specs=P(None, "pair", None, "virt"), check_vma=False
    )
```

```python
import jax
import jax.numpy as jnp
from jax import lax
from jax.experimental import pallas as pl
from jax.experimental.pallas import tpu as pltpu
from jax.sharding import PartitionSpec as P

AXES = ("pair", "virt")
F32, BF16 = jnp.float32, jnp.bfloat16
TOP = 1024.0
LANES = 128
ANY = pl.BlockSpec(memory_space=pl.ANY)
VMEM = pl.BlockSpec(memory_space=pltpu.VMEM)
SMEM = pl.BlockSpec(memory_space=pltpu.SMEM)


def dot(left, right):
    return jnp.dot(left, right, preferred_element_type=F32)


def iota(shape, axis):
    return lax.broadcasted_iota(jnp.int32, shape, axis)


def bound_at(block, at):
    return block[0:1, at : at + 1].astype(F32)


def with_bound(block, bound, at):
    here = (iota(block.shape, 0) == 0) & (iota(block.shape, 1) == at)
    return jnp.where(here, bound, block)


def sent_bound(bound):
    return jnp.maximum(bound * 1.01, 1e-35).astype(BF16).astype(F32)


def coded(values, bound):
    scaled = jnp.abs(values) * (TOP / bound)
    fourth = scaled * scaled
    fourth = fourth * fourth
    power = fourth * fourth * fourth
    return jnp.where(values < 0, -power, power)


def decoded(block, bound):
    power = block.astype(F32)
    magnitude = jnp.exp2(jnp.log2(jnp.maximum(jnp.abs(power), 1e-37)) * (1 / 12)) * (bound * (1 / TOP))
    return jnp.where(power == 0, 0.0, jnp.where(power < 0, -magnitude, magnitude))


def local(body, out_types, aligned, name, vmem=40):
    def kernel(index, *refs):
        results = body(index, *refs[: -len(out_types)])
        for ref, result in zip(refs[-len(out_types) :], results):
            if isinstance(result, list):
                for n, block in enumerate(result):
                    ref[n] = block.astype(ref.dtype)
            else:
                ref[...] = result.astype(ref.dtype)

    def call(index, *arrays):
        if not aligned:
            results = body(index, *arrays)
            results = [jnp.stack(result) if isinstance(result, list) else result for result in results]
            return [result.astype(kind.dtype) for result, kind in zip(results, out_types)]
        return pl.pallas_call(
            kernel,
            in_specs=[SMEM] + [VMEM] * len(arrays),
            out_specs=[VMEM] * len(out_types),
            out_shape=out_types,
            name=name,
            compiler_params=pltpu.CompilerParams(vmem_limit_bytes=vmem * 2**20),
        )(index, *arrays)

    return call


def product_kernel(same, depth, inner, virtuals, cols, nv):
    lane_tiles = -(-virtuals // LANES)
    half = depth // 2

    def lanes(tile):
        return min(LANES, virtuals - LANES * tile)

    def kernel(index, u_hbm, w_hbm, w_last, kept, sent, *scratch):
        bufs = list(scratch[: lane_tiles - 1]) + [w_last.reshape(depth * inner * 2, LANES)]
        us, first, second, out, sems, out_sems = (
            scratch[lane_tiles - 1 : lane_tiles + 1],
            *scratch[lane_tiles + 1 :],
        )
        w_rows = w_hbm.reshape(depth * inner * 2, virtuals)

        def u_copy(i, h):
            part = pl.ds(h * half, half)
            return pltpu.make_async_copy(u_hbm.at[i, part], us[i].at[part], sems.at[0, i, h])

        def w_copy(tile, h):
            part = pl.ds(h * half * inner * 2, half * inner * 2)
            return pltpu.make_async_copy(
                w_rows.at[part, pl.ds(LANES * tile, LANES)], bufs[tile].at[part], sems.at[1, tile, h]
            )

        order = ((0, 0), (1, 1)) if same else ((0, 1), (1, 0))
        lead = order[0][0]
        groups = [[("u", lead, h), ("w", 0, h), ("w", 1, h)] for h in range(2)]
        groups += [[("w", t, h) for t in (2 * n, 2 * n + 1) if t < lane_tiles - 1 for h in range(2)] for n in range(1, lane_tiles // 2)]
        groups += [[("u", 1 - lead, h)] for h in range(2)]
        copies = {key: (u_copy if key[0] == "u" else w_copy)(*key[1:]) for group in groups for key in group}
        state = {"started": 0, "waited": 0}

        def start_until(count):
            while state["started"] < min(count, len(groups)):
                for key in groups[state["started"]]:
                    copies[key].start()
                state["started"] += 1

        def need(group):
            while state["waited"] <= group:
                for key in groups[state["waited"]]:
                    copies[key].wait()
                state["waited"] += 1
                start_until(state["waited"] + 2)

        def weights(k, j, n):
            parts = [bufs[t][pl.ds(k * 2 * inner + j, inner, 2), :][:, : lanes(t)] for t in (2 * n, 2 * n + 1)]
            return jnp.concatenate(parts, axis=1)

        def product_tile(which, n):
            i, j = order[which]
            total = None
            for k in range(depth):
                if which == 0:
                    need(k // half if n == 0 else n + 1)
                elif n == 0:
                    need(len(groups) - 2 + k // half)
                term = dot(us[i][k], weights(k, j, n))
                total = term if total is None else total + term
            return total

        def place(v, rows, block):
            out[v, rows, :cols] = block
            return jnp.max(jnp.abs(block), axis=0, keepdims=True)

        start_until(2)
        largest = jnp.zeros((1, cols), F32)
        for n in range(lane_tiles // 2):
            tile = product_tile(0, n)
            first[:, 2 * LANES * n : 2 * LANES * n + tile.shape[1]] = tile

        def segment(v, tile, lower):
            big = jnp.zeros((1, cols), F32)
            begin, end = LANES * tile, LANES * tile + lanes(tile)
            on, past = v * cols, (v + 1) * cols
            flipped = {}

            def symmetric(source, r0, r1):
                if id(source) not in flipped:
                    flipped[id(source)] = source[on:past, begin:end].T
                return source[r0:r1, on:past] + flipped[id(source)][r0 - begin : r1 - begin]

            r0, r1 = begin, min(end, on)
            if not lower and r0 < r1:
                big = jnp.maximum(big, place(v, slice(r0, r1), symmetric(first, r0, r1)))
            r0, r1 = max(begin, on), min(end, past)
            if lower and r0 < r1:
                s00, s11 = symmetric(first, r0, r1), symmetric(second, r0, r1)
                a, b = r0 + iota(s00.shape, 0), on + iota(s00.shape, 1)
                big = jnp.maximum(big, place(v, slice(r0, r1), jnp.where(a <= b, s00, s11)))
                diagonal = jnp.sum(jnp.where(a == b, s11, 0.0), axis=1, keepdims=True)
                out[v, r0:r1, cols : cols + 1] = diagonal
                big = jnp.maximum(big, jnp.max(jnp.abs(diagonal)))
            r0, r1 = max(begin, past), end
            if lower and r0 < r1:
                big = jnp.maximum(big, place(v, slice(r0, r1), symmetric(second, r0, r1)))
            return big

        for n in range(lane_tiles // 2):
            tile = product_tile(1, n)
            second[:, 2 * LANES * n : 2 * LANES * n + tile.shape[1]] = tile
            for t in (2 * n, 2 * n + 1):
                rows = slice(LANES * t, LANES * t + lanes(t))
                for v in range(nv):
                    if same:
                        largest = jnp.maximum(largest, segment(v, t, False))
                    else:
                        block = first[rows, v * cols : (v + 1) * cols] + second[v * cols : (v + 1) * cols, rows].T
                        largest = jnp.maximum(largest, place(v, rows, block))
        if same:
            for t in range(lane_tiles):
                for v in range(nv):
                    largest = jnp.maximum(largest, segment(v, t, True))
        largest = jnp.max(largest)
        width = out.shape[-1] - cols
        for v in range(2):
            head = out[v, 0:8, cols:]
            here = (iota((8, width), 0) == 0) & (iota((8, width), 1) == 1)
            out[v, 0:8, cols:] = jnp.where(here, largest, head)
        for core in range(2):

            @pl.when(index[1] == core)
            def _():
                sends = []
                for x in range(nv // 2):
                    for slot, (target, v) in enumerate(((kept, 2 * x + core), (sent, 2 * x + 1 - core))):
                        sends.append(pltpu.make_async_copy(out.at[v], target.at[x], out_sems.at[x, slot]))
                for copy in sends:
                    copy.start()
                for copy in sends:
                    copy.wait()

    return kernel


def unique_sums(index, amplitudes, integrals, same, nv, width):
    _, depth, virtuals, inner = amplitudes.shape
    cols = virtuals // nv
    lane_tiles = -(-virtuals // LANES)
    half_type = jax.ShapeDtypeStruct((nv // 2, virtuals, width), F32)
    return pl.pallas_call(
        product_kernel(same, depth, inner, virtuals, cols, nv),
        grid=(1,),
        in_specs=[SMEM, ANY, ANY, pl.BlockSpec((depth, inner, 2, LANES), lambda _: (0, 0, 0, lane_tiles - 1))],
        out_specs=[ANY, ANY],
        out_shape=[half_type, half_type],
        scratch_shapes=[pltpu.VMEM((depth * inner * 2, LANES), BF16)] * (lane_tiles - 1)
        + [pltpu.VMEM((depth, virtuals, inner), BF16)] * 2
        + [pltpu.VMEM((virtuals, virtuals), F32)] * 2
        + [
            pltpu.VMEM((nv, virtuals, width), F32),
            pltpu.SemaphoreType.DMA((2, lane_tiles, 2)),
            pltpu.SemaphoreType.DMA((nv // 2, 2)),
        ],
        name="same" if same else "crossed",
        cost_estimate=pl.CostEstimate(
            flops=4 * depth * inner * virtuals * virtuals, bytes_accessed=4 * amplitudes.size, transcendentals=0
        ),
        compiler_params=pltpu.CompilerParams(vmem_limit_bytes=58 * 2**20),
    )(index, amplitudes, integrals, integrals)


def plain_sums(index, amplitudes, integrals, same, nv, width):
    virtuals = amplitudes.shape[2]
    cols = virtuals // nv

    def product(i, j):
        return jnp.einsum("kac,kcb->ab", amplitudes[i], integrals[:, :, j], preferred_element_type=F32)

    if same:
        s00, s11 = ((q + q.T) for q in (product(0, 0), product(1, 1)))
        a, b = (iota((virtuals, virtuals), axis) for axis in range(2))
        block, diagonal = jnp.where(a <= b, s00, s11), jnp.diagonal(s11)
    else:
        block, diagonal = product(0, 1) + product(1, 0).T, jnp.zeros((virtuals,), F32)
    largest = jnp.maximum(jnp.max(jnp.abs(block)), jnp.max(jnp.abs(diagonal)))
    parts = block.reshape(virtuals, nv, cols).transpose(1, 0, 2)
    extra = jnp.stack([diagonal, jnp.full((virtuals,), largest)], axis=1)
    extra = jnp.pad(extra, ((0, 0), (0, width - cols - 2)))
    parts = jnp.concatenate([parts, jnp.broadcast_to(extra, (nv, *extra.shape))], axis=2)
    parts = parts.reshape(nv // 2, 2, virtuals, width)
    return [lax.dynamic_index_in_dim(parts, c, 1, keepdims=False) for c in (index[1], 1 - index[1])]


def solution(mesh):
    np_, nv = mesh.shape["pair"], mesh.shape["virt"]
    nx, nz, ratio = nv // 2, np_ // 2, np_ // nv

    def send(block, move):
        pairs = []
        for p in range(np_):
            for v in range(nv):
                q, w = move(p, v)
                pairs.append((p * nv + v, q * nv + w))
        return lax.ppermute(block, AXES, pairs)

    def shards(amplitudes, integrals):
        _, _, virtuals, inner = amplitudes.shape
        rows, cols = virtuals // np_, virtuals // nv
        width = -(-(cols + 2) // LANES) * LANES
        at = cols + 1
        aligned = rows % 8 == 0 and inner % 16 == 0 and virtuals % 64 == 0
        p, v = lax.axis_index("pair"), lax.axis_index("virt")
        index = jnp.stack([v // 2, v % 2, p // 2, p % 2, p, v]).astype(jnp.int32)
        steps = [(dx, dy) for dx in range(nx) for dy in range(2) if dx or dy]

        def chip_sum(index, kept, came):
            x, y = index[0], index[3]
            bound = sent_bound(bound_at(kept[0, 0, 0], at) + bound_at(came[0, 0, 0], at))

            def block(x_at, y_at, z):
                return kept[x_at, z, y_at] + came[x_at, z, y_at]

            own = [block(x, y, z) for z in range(nz)]
            results = [[with_bound(own[0], bound, at)] + own[1:]]
            for dx, dy in steps:
                blocks = [coded(block((x + dx) % nx, (y + dy) % 2, z), bound) for z in range(nz)]
                results.append([with_bound(blocks[0], bound, at)] + blocks[1:])
            return results

        def plane_sum(index, own, *came):
            z_own = index[2]
            bounds = [bound_at(array[0], at) for array in came]
            bound = sent_bound(sum(bounds, bound_at(own[0], at)))

            def block(z):
                total = own[z]
                for array, of in zip(came, bounds):
                    total = total + decoded(array[z], of)
                return total

            results = [with_bound(block(z_own), bound, at)]
            for dz in range(1, nz):
                results.append(with_bound(coded(block((z_own + dz) % nz), bound), bound, at))
            return results

        def line_sum(index, own, *came):
            total = own[...]
            for array in came:
                array = array[...]
                total = total + decoded(array, bound_at(array, at))
            flipped = [total[:, h * rows : (h + 1) * rows].T for h in range(ratio)]
            results = [total]
            for t in range(ratio):
                tile = flipped[0]
                for h in range(1, ratio):
                    tile = jnp.where((index[4] + t) % ratio == h, flipped[h], tile)
                results.append(tile)
            return results

        def outcome(index, crossed, same, *came):
            def mirrored(tiles):
                parts = []
                for h in range(ratio):
                    part = tiles[0][...]
                    for t in range(1, ratio):
                        part = jnp.where((index[4] + ratio - h) % ratio == t, tiles[t][...], part)
                    parts.append(part)
                return jnp.concatenate(parts, axis=1) if ratio > 1 else parts[0]

            same = same[...]
            square = same[:, :cols]
            other = mirrored(came[ratio:])
            a = index[4] * rows + iota(square.shape, 0)
            b = index[5] * cols + iota(square.shape, 1)
            out00 = jnp.where(a <= b, square, other)
            out11 = jnp.where(a > b, square, jnp.where(a == b, same[:, cols : cols + 1], other))
            return [out00, crossed[...][:, :cols], mirrored(came[:ratio]), out11]

        def outcome_kernel(index, *refs):
            for n, block in enumerate(outcome(index, *refs[:-1])):
                refs[-1][n // 2, :, n % 2, :] = block

        def kind(shape, dtype=F32):
            return jax.ShapeDtypeStruct(shape, dtype)

        def reduced(same):
            sums = unique_sums if aligned else plain_sums
            kept, other = sums(index, amplitudes, integrals, same, nv, width)
            came = send(other, lambda p, v: (p, v ^ 1))
            shape = (nx, nz, 2, rows, width)
            types = [kind((nz, rows, width))] + [kind((nz, rows, width), BF16)] * len(steps)
            own, *outs = local(chip_sum, types, aligned, "chip_sum")(index, kept.reshape(shape), came.reshape(shape))
            came = [send(block, lambda p, v: (p ^ dy, (v + 2 * dx) % nv)) for (dx, dy), block in zip(steps, outs)]
            types = [kind((rows, width))] + [kind((rows, width), BF16)] * (nz - 1)
            own, *outs = local(plane_sum, types, aligned, "plane_sum")(index, own, *came)
            came = [send(block, lambda p, v: ((p + 2 * dz) % np_, v)) for dz, block in zip(range(1, nz), outs)]
            types = [kind((rows, width))] + [kind((rows, rows))] * ratio
            total, *tiles = local(line_sum, types, aligned, "line_sum")(index, own, *came)
            return total, [
                send(tile, lambda p, v: (ratio * v + (p % ratio + t) % ratio, p // ratio)) for t, tile in enumerate(tiles)
            ]

        crossed, crossed_tiles = reduced(False)
        same, same_tiles = reduced(True)
        arrays = [crossed, same, *crossed_tiles, *same_tiles]
        if not aligned:
            blocks = outcome(index, *arrays)
            return jnp.stack([jnp.stack(blocks[:2], 1), jnp.stack(blocks[2:], 1)])
        return pl.pallas_call(
            outcome_kernel,
            in_specs=[SMEM] + [VMEM] * len(arrays),
            out_specs=VMEM,
            out_shape=kind((2, rows, 2, cols)),
            name="outcome",
        )(index, *arrays)

    placed = (P(None, "pair", None, "virt"), P("pair", "virt", None, None))
    return jax.shard_map(
        shards, mesh=mesh, in_specs=placed, out_specs=P(None, "pair", None, "virt"), check_vma=False
    )
```

```python
import math

import jax
import jax.numpy as jnp
from jax import lax
from jax.experimental import pallas as pl
from jax.experimental.pallas import tpu as pltpu
from jax.sharding import PartitionSpec as P

AXES = ("pair", "virt")
F32, BF16 = jnp.float32, jnp.bfloat16
TOP = 1024.0
LANES = 128
ANY = pl.BlockSpec(memory_space=pl.ANY)
VMEM = pl.BlockSpec(memory_space=pltpu.VMEM)
SMEM = pl.BlockSpec(memory_space=pltpu.SMEM)


def dot(left, right):
    return jnp.dot(left, right, preferred_element_type=F32)


def iota(shape, axis):
    return lax.broadcasted_iota(jnp.int32, shape, axis)


def bound_at(block, at):
    return block[0:1, at : at + 1].astype(F32)


def with_bound(block, bound, at):
    here = (iota(block.shape, 0) == 0) & (iota(block.shape, 1) == at)
    return jnp.where(here, bound, block)


def sent_bound(bound):
    return jnp.maximum(bound * 1.01, 1e-35).astype(BF16).astype(F32)


def coded(values, bound):
    scaled = jnp.abs(values) * (TOP / bound)
    fourth = scaled * scaled
    fourth = fourth * fourth
    power = fourth * fourth * fourth
    return jnp.where(values < 0, -power, power)


def decoded(block, bound):
    power = block.astype(F32)
    magnitude = jnp.exp2(jnp.log2(jnp.maximum(jnp.abs(power), 1e-37)) * (1 / 12)) * (bound * (1 / TOP))
    return jnp.where(power == 0, 0.0, jnp.where(power < 0, -magnitude, magnitude))


def local(body, out_types, aligned, name, cost=0):
    def kernel(index, *refs):
        results = body(index, *refs[: -len(out_types)])
        for ref, result in zip(refs[-len(out_types) :], results):
            if isinstance(result, list):
                for n, block in enumerate(result):
                    ref[n] = block.astype(ref.dtype)
            else:
                ref[...] = result.astype(ref.dtype)

    def call(index, *arrays):
        if not aligned:
            results = body(index, *arrays)
            results = [jnp.stack(result) if isinstance(result, list) else result for result in results]
            return [result.astype(kind.dtype) for result, kind in zip(results, out_types)]
        return pl.pallas_call(
            kernel,
            in_specs=[SMEM] + [VMEM] * len(arrays),
            out_specs=[VMEM] * len(out_types),
            out_shape=out_types,
            name=name,
            cost_estimate=pl.CostEstimate(flops=cost, bytes_accessed=2**20, transcendentals=0),
            compiler_params=pltpu.CompilerParams(vmem_limit_bytes=4 * 2**20),
        )(index, *arrays)

    return call


def lane_tiles(virtuals):
    return -(-virtuals // LANES)


def lanes(tile, virtuals):
    return min(LANES, virtuals - LANES * tile)


def product(u, w, i, j, rows, n):
    _, depth, virtuals, inner = u.shape
    total = None
    for k in range(depth):
        parts = [
            w[pl.ds((t * depth + k) * 2 * inner + j, inner, 2), :][:, : lanes(t, virtuals)]
            for t in (2 * n, 2 * n + 1)
        ]
        term = dot(u[i, k, rows, :], jnp.concatenate(parts, axis=1))
        total = term if total is None else total + term
    return total


def pair_of_tiles(n, virtuals):
    return slice(2 * LANES * n, min(2 * LANES * (n + 1), virtuals))


def brought(u_hbm, w_hbm, u, w, sems):
    _, depth, virtuals, inner = u_hbm.shape
    tiles = lane_tiles(virtuals)
    w_rows = w_hbm.reshape(depth * inner * 2, virtuals)

    def u_copies(i):
        return [pltpu.make_async_copy(u_hbm.at[i, k], u.at[i, k], sems.at[i, k]) for k in range(depth)]

    def tile_rows(tile):
        return pl.ds(tile * depth * inner * 2, depth * inner * 2)

    def w_copy(tile):
        source = w_rows.at[:, pl.ds(LANES * tile, LANES)]
        return pltpu.make_async_copy(source, w.at[tile_rows(tile)], sems.at[2, tile])

    def last_tile(block):
        w[tile_rows(tiles - 1), :] = block.reshape(depth * inner * 2, LANES)[...]

    groups = [
        u_copies(1) + [w_copy(tile) for tile in range(2)],
        [w_copy(tile) for tile in range(2, tiles - 1)],
        u_copies(0),
    ]

    def start(group):
        for copy in groups[group]:
            copy.start()

    def wait(group):
        for copy in groups[group]:
            copy.wait()

    start(0)
    pltpu.emit_pipeline(
        last_tile,
        grid=(1,),
        in_specs=[pl.BlockSpec((depth, inner, 2, LANES), lambda _: (0, 0, 0, tiles - 1))],
    )(w_hbm)
    return start, wait


class Half:
    def __init__(self, out, low, cols):
        self.out, self.low, self.cols = out, low, cols
        self.high = low + out.shape[1]
        self.largest = jnp.zeros((1, cols), F32)

    def place(self, v, r0, r1, block):
        self.out[v, r0 - self.low : r1 - self.low, : self.cols] = block
        self.largest = jnp.maximum(self.largest, jnp.max(jnp.abs(block), axis=0, keepdims=True))

    def finish(self, index, kept, sent):
        out, cols = self.out, self.cols
        largest = jnp.max(self.largest)
        for v in range(2):
            head = out[v, 0:8, cols:]
            here = (iota(head.shape, 0) == 0) & (iota(head.shape, 1) == 1)
            out[v, 0:8, cols:] = jnp.where(here, largest, head)
        for core in range(2):

            @pl.when(index[1] == core)
            def _():
                for x in range(kept.shape[0]):
                    kept[x] = out[2 * x + core]
                    sent[x] = out[2 * x + 1 - core]


def crossed_kernel(cols):
    def kernel(index, u_hbm, w_hbm, kept, sent, u, w, other, own, out, sems):
        virtuals = u.shape[2]
        tiles = lane_tiles(virtuals)
        start, wait = brought(u_hbm, w_hbm, u, w, sems)
        half = Half(out, 0, cols)
        everything = slice(0, virtuals)
        wait(0)
        start(1)
        other[:, pair_of_tiles(0, virtuals)] = product(u, w, 1, 0, everything, 0)
        wait(1)
        start(2)
        for n in range(1, tiles // 2):
            other[:, pair_of_tiles(n, virtuals)] = product(u, w, 1, 0, everything, n)
        wait(2)
        v = 0
        for n in range(tiles // 2):
            columns = pair_of_tiles(n, virtuals)
            own[:, columns] = product(u, w, 0, 1, everything, n)
            while (v + 1) * cols <= columns.stop:
                on, past = v * cols, (v + 1) * cols
                for t in range(tiles):
                    r0, r1 = LANES * t, LANES * t + lanes(t, virtuals)
                    half.place(v, r0, r1, own[r0:r1, on:past] + other[on:past, r0:r1].T)
                v += 1
        half.finish(index, kept, sent)

    return kernel


def first_square_kernel(index, u, w, square):
    virtuals = u.shape[2]
    for n in range(lane_tiles(virtuals) // 2):
        square[:, pair_of_tiles(n, virtuals)] = product(u, w, 0, 0, slice(0, virtuals // 2), n)


def other_squares_kernel(index, u, w, rest, square):
    virtuals = u.shape[2]
    for n in range(lane_tiles(virtuals) // 2):
        rest[:, pair_of_tiles(n, virtuals)] = product(u, w, 0, 0, slice(virtuals // 2, virtuals), n)
        square[:, pair_of_tiles(n, virtuals)] = product(u, w, 1, 1, slice(0, virtuals), n)


def same_kernel(cols):
    def kernel(index, p00, p00_rest, p11, kept, sent, out):
        virtuals = p11.shape[0]
        middle, tiles, nv = virtuals // 2, lane_tiles(virtuals), virtuals // cols
        half = Half(out, 0, cols)

        def rows_of(i, r0, r1, c0, c1):
            if i == 1:
                return p11[r0:r1, c0:c1]
            if r1 <= middle:
                return p00[r0:r1, c0:c1]
            if r0 >= middle:
                return p00_rest[r0 - middle : r1 - middle, c0:c1]
            return jnp.concatenate([p00[r0:middle, c0:c1], p00_rest[0 : r1 - middle, c0:c1]], axis=0)

        def segment(v, tile):
            begin, end = LANES * tile, LANES * tile + lanes(tile, virtuals)
            on, past = v * cols, (v + 1) * cols
            flips = {}

            def symmetric(i, r0, r1):
                if i not in flips:
                    flips[i] = rows_of(i, on, past, begin, end).T
                return rows_of(i, r0, r1, on, past) + flips[i][r0 - begin : r1 - begin]

            r0, r1 = begin, min(end, on)
            if r0 < r1:
                half.place(v, r0, r1, symmetric(0, r0, r1))
            r0, r1 = max(begin, on), min(end, past)
            if r0 < r1:
                s00, s11 = symmetric(0, r0, r1), symmetric(1, r0, r1)
                a, b = r0 + iota(s00.shape, 0), on + iota(s00.shape, 1)
                half.place(v, r0, r1, jnp.where(a <= b, s00, s11))
                diagonal = jnp.where(a == b, s11, 0.0)
                out[v, r0:r1, cols : cols + 1] = jnp.sum(diagonal, axis=1, keepdims=True)
                half.largest = jnp.maximum(half.largest, jnp.max(jnp.abs(diagonal), axis=0, keepdims=True))
            r0, r1 = max(begin, past), end
            if r0 < r1:
                half.place(v, r0, r1, symmetric(1, r0, r1))

        for v in range(nv):
            for t in range(tiles):
                segment(v, t)
        half.finish(index, kept, sent)

    return kernel


def on_chip(body, name, out_shape, scratch, flops, index, u, w, *arrays):
    ins = 3 + len(arrays)
    outs = ins + len(out_shape)

    def kernel(*refs):
        body(*refs[:outs], *refs[outs + 2 :])

    *results, u, w = pl.pallas_call(
        kernel,
        in_specs=[SMEM] + [VMEM] * (ins - 1),
        out_specs=[VMEM] * (len(out_shape) + 2),
        out_shape=[*out_shape, jax.ShapeDtypeStruct(u.shape, u.dtype), jax.ShapeDtypeStruct(w.shape, w.dtype)],
        input_output_aliases={1: len(out_shape), 2: len(out_shape) + 1},
        scratch_shapes=[pltpu.VMEM(shape, F32) for shape in scratch],
        name=name,
        cost_estimate=pl.CostEstimate(flops=flops, bytes_accessed=2**20, transcendentals=0),
        compiler_params=pltpu.CompilerParams(vmem_limit_bytes=5 * 2**20),
    )(index, u, w, *arrays)
    return results, u, w


def crossed_sums(index, amplitudes, integrals, half_types, cols):
    _, depth, virtuals, inner = amplitudes.shape
    tiles = lane_tiles(virtuals)
    width, nv = half_types[0].shape[-1], virtuals // cols
    kept, sent, u, w = pl.pallas_call(
        crossed_kernel(cols),
        in_specs=[SMEM, ANY, ANY],
        out_specs=[VMEM] * 4,
        out_shape=[
            *half_types,
            jax.ShapeDtypeStruct(amplitudes.shape, BF16),
            jax.ShapeDtypeStruct((tiles * depth * inner * 2, LANES), BF16),
        ],
        scratch_shapes=[
            pltpu.VMEM((virtuals, virtuals), F32),
            pltpu.VMEM((virtuals, virtuals), F32),
            pltpu.VMEM((nv, virtuals, width), F32),
            pltpu.SemaphoreType.DMA((3, max(depth, tiles))),
        ],
        name="crossed",
        cost_estimate=pl.CostEstimate(
            flops=4 * depth * inner * virtuals * virtuals, bytes_accessed=4 * amplitudes.size, transcendentals=0
        ),
        compiler_params=pltpu.CompilerParams(vmem_limit_bytes=20 * 2**20),
    )(index, amplitudes, integrals)
    return (kept, sent), u, w


def after(value, *others):
    return lax.optimization_barrier((value, *others))[0]


def plain_sums(index, amplitudes, integrals, same, nv, width):
    virtuals = amplitudes.shape[2]
    cols = virtuals // nv

    def cycle(i, j):
        return jnp.einsum("kac,kcb->ab", amplitudes[i], integrals[:, :, j], preferred_element_type=F32)

    if same:
        s00, s11 = ((q + q.T) for q in (cycle(0, 0), cycle(1, 1)))
        a, b = (iota((virtuals, virtuals), axis) for axis in range(2))
        block, diagonal = jnp.where(a <= b, s00, s11), jnp.diagonal(s11)
    else:
        block, diagonal = cycle(0, 1) + cycle(1, 0).T, jnp.zeros((virtuals,), F32)
    largest = jnp.maximum(jnp.max(jnp.abs(block)), jnp.max(jnp.abs(diagonal)))
    parts = block.reshape(virtuals, nv, cols).transpose(1, 0, 2)
    extra = jnp.stack([diagonal, jnp.full((virtuals,), largest)], axis=1)
    extra = jnp.pad(extra, ((0, 0), (0, width - cols - 2)))
    parts = jnp.concatenate([parts, jnp.broadcast_to(extra, (nv, *extra.shape))], axis=2)
    parts = parts.reshape(nv // 2, 2, virtuals, width)
    return [lax.dynamic_index_in_dim(parts, c, 1, keepdims=False) for c in (index[1], 1 - index[1])]


def solution(mesh):
    np_, nv = mesh.shape["pair"], mesh.shape["virt"]
    nx, nz, ratio = nv // 2, np_ // 2, np_ // nv

    def send(block, move):
        pairs = []
        for p in range(np_):
            for v in range(nv):
                q, w = move(p, v)
                pairs.append((p * nv + v, q * nv + w))
        return lax.ppermute(block, AXES, pairs)

    def shards(amplitudes, integrals):
        _, _, virtuals, inner = amplitudes.shape
        rows, cols = virtuals // np_, virtuals // nv
        width = -(-(cols + 2) // LANES) * LANES
        at = cols + 1
        aligned = rows % 8 == 0 and inner % 16 == 0 and virtuals % 64 == 0
        p, v = lax.axis_index("pair"), lax.axis_index("virt")
        index = jnp.stack([v // 2, v % 2, p // 2, p % 2, p, v]).astype(jnp.int32)
        steps = [(dx, dy) for dx in range(nx) for dy in range(2) if dx or dy]

        def chip_sum(index, kept, came):
            x, y = index[0], index[3]
            bound = sent_bound(bound_at(kept[0, 0, 0], at) + bound_at(came[0, 0, 0], at))

            def block(x_at, y_at, z):
                return kept[x_at, z, y_at] + came[x_at, z, y_at]

            own = [block(x, y, z) for z in range(nz)]
            results = [[with_bound(own[0], bound, at)] + own[1:]]
            for dx, dy in steps:
                blocks = [coded(block((x + dx) % nx, (y + dy) % 2, z), bound) for z in range(nz)]
                results.append([with_bound(blocks[0], bound, at)] + blocks[1:])
            return results

        def plane_sum(index, own, *came):
            z_own = index[2]
            bounds = [bound_at(array[0], at) for array in came]
            bound = sent_bound(sum(bounds, bound_at(own[0], at)))

            def block(z):
                total = own[z]
                for array, of in zip(came, bounds):
                    total = total + decoded(array[z], of)
                return total

            results = [block(z_own)]
            for dz in range(1, nz):
                results.append(with_bound(coded(block((z_own + dz) % nz), bound), bound, at))
            return results

        def line_sum(count, paired):
            def body(index, own, *arrays):
                total = own[...]
                for array in arrays[:count]:
                    array = array[...]
                    total = total + decoded(array, bound_at(array, at))
                flipped = [total[:, h * rows : (h + 1) * rows].T for h in range(ratio)]
                results = [total]
                for t in range(ratio):
                    tile = flipped[0]
                    for h in range(1, ratio):
                        tile = jnp.where((index[4] + t) % ratio == h, flipped[h], tile)
                    results.append([arrays[count + t][...], tile] if paired else tile)
                return results

            return body

        def outcome(index, crossed, same, *came):
            def mirrored(which):
                parts = []
                for h in range(ratio):
                    part = came[0][which]
                    for t in range(1, ratio):
                        part = jnp.where((index[4] + ratio - h) % ratio == t, came[t][which], part)
                    parts.append(part)
                return jnp.concatenate(parts, axis=1) if ratio > 1 else parts[0]

            same = same[...]
            square = same[:, :cols]
            other = mirrored(1)
            a = index[4] * rows + iota(square.shape, 0)
            b = index[5] * cols + iota(square.shape, 1)
            out00 = jnp.where(a <= b, square, other)
            out11 = jnp.where(a > b, square, jnp.where(a == b, same[:, cols : cols + 1], other))
            return [out00, crossed[...][:, :cols], mirrored(0), out11]

        def outcome_kernel(index, *refs):
            for n, block in enumerate(outcome(index, *refs[:-1])):
                refs[-1][n // 2, :, n % 2, :] = block

        def kind(shape, dtype=F32):
            return jax.ShapeDtypeStruct(shape, dtype)

        work = amplitudes.size * virtuals

        def across_core(pair_of):
            return pair_of[0], send(pair_of[1], lambda p, v: (p, v ^ 1))

        def across_plane(index, kept, came):
            shape = (nx, nz, 2, rows, width)
            types = [kind((nz, rows, width))] + [kind((nz, rows, width), BF16)] * len(steps)
            own, *outs = local(chip_sum, types, aligned, "chip_sum", work)(index, kept.reshape(shape), came.reshape(shape))
            came = [send(block, lambda p, v: (p ^ dy, (v + 2 * dx) % nv)) for (dx, dy), block in zip(steps, outs)]
            return own, came

        def across_line(index, own, came):
            types = [kind((rows, width))] + [kind((rows, width), BF16)] * (nz - 1)
            own, *outs = local(plane_sum, types, aligned, "plane_sum", 2 * work)(index, own, *came)
            return own, [send(block, lambda p, v: ((p + 2 * dz) % np_, v)) for dz, block in zip(range(1, nz), outs)]

        def line_total(index, own, came, first_tiles=()):
            shape = (2, rows, rows) if first_tiles else (rows, rows)
            types = [kind((rows, width))] + [kind(shape)] * ratio
            body = line_sum(len(came), bool(first_tiles))
            return local(body, types, aligned, "line_sum")(index, own, *came, *first_tiles)

        def exchanged(tiles):
            return [
                send(tile, lambda p, v: (ratio * v + (p % ratio + t) % ratio, p // ratio)) for t, tile in enumerate(tiles)
            ]

        if aligned:
            half_types = [kind((nx, virtuals, width))] * 2
            crossed, u, w = crossed_sums(index, amplitudes, integrals, half_types, cols)
            crossed = across_core(crossed)
            square = kind((virtuals // 2, virtuals))
            (p00,), u, w = on_chip(
                first_square_kernel, "first_square", [square], [], work // 2, after(index, crossed[0]), u, w
            )
            crossed = across_plane(after(index, p00), *crossed)
            (p00_rest, p11), u, w = on_chip(
                other_squares_kernel,
                "other_squares",
                [square, kind((virtuals, virtuals))],
                [],
                3 * work // 2,
                after(index, crossed[0]),
                u,
                w,
            )
            crossed = across_line(after(index, p11), *crossed)
            same = pl.pallas_call(
                same_kernel(cols),
                in_specs=[SMEM] + [VMEM] * 3,
                out_specs=[VMEM] * 2,
                out_shape=half_types,
                scratch_shapes=[pltpu.VMEM((nv, virtuals, width), F32)],
                name="same",
                cost_estimate=pl.CostEstimate(flops=work // 2, bytes_accessed=2**20, transcendentals=0),
                compiler_params=pltpu.CompilerParams(vmem_limit_bytes=9 * 2**20),
            )(after(index, crossed[0]), p00, p00_rest, p11)
            same = across_core(same)
            same = across_plane(index, *same)
            crossed, *tiles = line_total(after(index, same[0]), *crossed)
            same = across_line(after(index, crossed), *same)
        else:
            crossed, same = (
                across_line(index, *across_plane(index, *across_core(plain_sums(index, amplitudes, integrals, kind_same, nv, width))))
                for kind_same in (False, True)
            )
            crossed, *tiles = line_total(index, *crossed)
        same, *tiles = line_total(index, *same, tiles)
        arrays = [crossed, same, *exchanged(tiles)]
        if not aligned:
            blocks = outcome(index, *arrays)
            return jnp.stack([jnp.stack(blocks[:2], 1), jnp.stack(blocks[2:], 1)])
        return pl.pallas_call(
            outcome_kernel,
            in_specs=[SMEM] + [VMEM] * len(arrays),
            out_specs=VMEM,
            out_shape=kind((2, rows, 2, cols)),
            name="outcome",
            compiler_params=pltpu.CompilerParams(vmem_limit_bytes=8 * 2**20),
        )(index, *arrays)

    placed = (P(None, "pair", None, "virt"), P("pair", "virt", None, None))
    return jax.shard_map(
        shards, mesh=mesh, in_specs=placed, out_specs=P(None, "pair", None, "virt"), check_vma=False
    )
```

```python
import math

import jax
import jax.numpy as jnp
from jax import lax
from jax.experimental import pallas as pl
from jax.experimental.pallas import tpu as pltpu
from jax.sharding import PartitionSpec as P

AXES = ("pair", "virt")
F32, BF16 = jnp.float32, jnp.bfloat16
TOP = 1024.0
LANES = 128
ANY = pl.BlockSpec(memory_space=pl.ANY)
VMEM = pl.BlockSpec(memory_space=pltpu.VMEM)
SMEM = pl.BlockSpec(memory_space=pltpu.SMEM)


def dot(left, right):
    return jnp.dot(left, right, preferred_element_type=F32)


def iota(shape, axis):
    return lax.broadcasted_iota(jnp.int32, shape, axis)


def bound_at(block, at):
    return block[0:1, at : at + 1].astype(F32)


def with_bound(block, bound, at):
    here = (iota(block.shape, 0) == 0) & (iota(block.shape, 1) == at)
    return jnp.where(here, bound, block)


def sent_bound(bound):
    return jnp.maximum(bound * 1.01, 1e-35).astype(BF16).astype(F32)


def coded(values, bound):
    scaled = jnp.abs(values) * (TOP / bound)
    fourth = scaled * scaled
    fourth = fourth * fourth
    power = fourth * fourth * fourth
    return jnp.where(values < 0, -power, power)


def decoded(block, bound):
    power = block.astype(F32)
    magnitude = jnp.exp2(jnp.log2(jnp.maximum(jnp.abs(power), 1e-37)) * (1 / 12)) * (bound * (1 / TOP))
    return jnp.where(power == 0, 0.0, jnp.where(power < 0, -magnitude, magnitude))


def local(body, out_types, aligned, name, cost=0):
    def kernel(index, *refs):
        results = body(index, *refs[: -len(out_types)])
        for ref, result in zip(refs[-len(out_types) :], results):
            if isinstance(result, list):
                for n, block in enumerate(result):
                    ref[n] = block.astype(ref.dtype)
            else:
                ref[...] = result.astype(ref.dtype)

    def call(index, *arrays):
        if not aligned:
            results = body(index, *arrays)
            results = [jnp.stack(result) if isinstance(result, list) else result for result in results]
            return [result.astype(kind.dtype) for result, kind in zip(results, out_types)]
        return pl.pallas_call(
            kernel,
            in_specs=[SMEM] + [VMEM] * len(arrays),
            out_specs=[VMEM] * len(out_types),
            out_shape=out_types,
            name=name,
            cost_estimate=pl.CostEstimate(flops=cost, bytes_accessed=2**20, transcendentals=0),
            compiler_params=pltpu.CompilerParams(vmem_limit_bytes=2 * 2**20),
        )(index, *arrays)

    return call


def lane_tiles(virtuals):
    return -(-virtuals // LANES)


def lanes(tile, virtuals):
    return min(LANES, virtuals - LANES * tile)


def product(u, w, i, j, rows, n, ks=None):
    _, depth, virtuals, inner = u.shape
    total = None
    for k in ks or range(depth):
        parts = [
            w[pl.ds((t * depth + k) * 2 * inner + j, inner, 2), :][:, : lanes(t, virtuals)]
            for t in (2 * n, 2 * n + 1)
        ]
        term = dot(u[i, k, rows, :], jnp.concatenate(parts, axis=1))
        total = term if total is None else total + term
    return total


def pair_of_tiles(n, virtuals):
    return slice(2 * LANES * n, min(2 * LANES * (n + 1), virtuals))


class Half:
    def __init__(self, out, low, cols):
        self.out, self.low, self.cols = out, low, cols
        self.high = low + out.shape[1]
        self.largest = jnp.zeros((1, cols), F32)

    def place(self, v, r0, r1, block):
        self.out[v, r0 - self.low : r1 - self.low, : self.cols] = block
        self.largest = jnp.maximum(self.largest, jnp.max(jnp.abs(block), axis=0, keepdims=True))

    def finish(self, index, kept, sent):
        out, cols = self.out, self.cols
        largest = jnp.max(self.largest)
        for v in range(2):
            head = out[v, 0:8, cols:]
            here = (iota(head.shape, 0) == 0) & (iota(head.shape, 1) == 1)
            out[v, 0:8, cols:] = jnp.where(here, largest, head)
        for core in range(2):

            @pl.when(index[1] == core)
            def _():
                for x in range(kept.shape[0]):
                    kept[x] = out[2 * x + core]
                    sent[x] = out[2 * x + 1 - core]


def crossed_kernel(cols):
    def kernel(index, u_hbm, w_hbm, kept, sent, u, w, other, own, out, ring, u_sems, w_sems):
        _, depth, virtuals, inner = u.shape
        tiles, slots = lane_tiles(virtuals), ring.shape[0]
        everything, pairs = slice(0, virtuals), tiles // 2
        half = Half(out, 0, cols)

        def u_copy(i, k):
            return pltpu.make_async_copy(u_hbm.at[i, k], u.at[i, k], u_sems.at[i, k])

        def w_copy(k):
            source = w_hbm.at[k].reshape(2 * inner, virtuals)
            return pltpu.make_async_copy(source, ring.at[k % slots], w_sems.at[k])

        def take(k):
            w_copy(k).wait()
            for t in range(tiles):
                rows = slice((t * depth + k) * 2 * inner, (t * depth + k + 1) * 2 * inner)
                width = lanes(t, virtuals)
                w[rows, :width] = ring[k % slots, :, LANES * t : LANES * t + width]
            if k + slots < depth:
                w_copy(k + slots).start()

        cuts = [0, 2 * depth // 7, 9 * depth // 14, depth]
        parts = [range(*cuts[n : n + 2]) for n in range(3)]
        for k in range(slots):
            w_copy(k).start()
        for k in parts[0]:
            u_copy(1, k).start()
        for number, ks in enumerate(parts):
            for k in ks:
                take(k)
            for k in ks:
                u_copy(1, k).wait()
            for k in parts[number + 1] if number < 2 else range(depth):
                u_copy(1 if number < 2 else 0, k).start()
            for n in range(pairs):
                term = product(u, w, 1, 0, everything, n, ks)
                columns = pair_of_tiles(n, virtuals)
                other[:, columns] = term if number == 0 else other[:, columns] + term
        for k in range(depth):
            u_copy(0, k).wait()
        v, wide = 0, 2 * LANES
        for n in range(pairs):
            columns = pair_of_tiles(n, virtuals)
            if n:
                own[:, :wide] = own[:, wide:]
            own[:, wide : wide + columns.stop - columns.start] = product(u, w, 0, 1, everything, n)
            while (v + 1) * cols <= columns.stop:
                on, past = v * cols, (v + 1) * cols
                shift = wide - columns.start
                for t in range(tiles):
                    r0, r1 = LANES * t, LANES * t + lanes(t, virtuals)
                    half.place(v, r0, r1, own[r0:r1, on + shift : past + shift] + other[on:past, r0:r1].T)
                v += 1
        half.finish(index, kept, sent)

    return kernel


def first_square_kernel(index, u, w, square):
    virtuals = u.shape[2]
    for n in range(lane_tiles(virtuals) // 2):
        square[:, pair_of_tiles(n, virtuals)] = product(u, w, 0, 0, slice(0, virtuals // 2), n)


class Triangles:
    def __init__(self, half, p00, p00_rest, p11, virtuals):
        self.half, self.p00, self.p00_rest, self.p11, self.virtuals = half, p00, p00_rest, p11, virtuals

    def rows_of(self, i, r0, r1, c0, c1):
        middle = self.virtuals // 2
        if i == 1:
            return self.p11[r0:r1, c0:c1]
        if r1 <= middle:
            return self.p00[r0:r1, c0:c1]
        if r0 >= middle:
            return self.p00_rest[r0 - middle : r1 - middle, c0:c1]
        return jnp.concatenate([self.p00[r0:middle, c0:c1], self.p00_rest[0 : r1 - middle, c0:c1]], axis=0)

    def place(self, v, tile, above):
        half, cols = self.half, self.half.cols
        begin, end = LANES * tile, LANES * tile + lanes(tile, self.virtuals)
        on, past = v * cols, (v + 1) * cols
        flips = {}

        def symmetric(i, r0, r1):
            if i not in flips:
                flips[i] = self.rows_of(i, on, past, begin, end).T
            return self.rows_of(i, r0, r1, on, past) + flips[i][r0 - begin : r1 - begin]

        r0, r1 = begin, min(end, on)
        if above and r0 < r1:
            half.place(v, r0, r1, symmetric(0, r0, r1))
        r0, r1 = max(begin, on), min(end, past)
        if not above and r0 < r1:
            s00, s11 = symmetric(0, r0, r1), symmetric(1, r0, r1)
            a, b = r0 + iota(s00.shape, 0), on + iota(s00.shape, 1)
            half.place(v, r0, r1, jnp.where(a <= b, s00, s11))
            diagonal = jnp.where(a == b, s11, 0.0)
            half.out[v, r0:r1, cols : cols + 1] = jnp.sum(diagonal, axis=1, keepdims=True)
            half.largest = jnp.maximum(half.largest, jnp.max(jnp.abs(diagonal), axis=0, keepdims=True))
        r0, r1 = max(begin, past), end
        if not above and r0 < r1:
            half.place(v, r0, r1, symmetric(1, r0, r1))


def other_squares_kernel(cols):
    def kernel(index, u, w, p00, p00_rest, p11, out, largest):
        virtuals = u.shape[2]
        tiles, nv = lane_tiles(virtuals), virtuals // cols
        half = Half(out, 0, cols)
        triangles = Triangles(half, p00, p00_rest, p11, virtuals)
        for n in range(tiles // 2):
            p00_rest[:, pair_of_tiles(n, virtuals)] = product(u, w, 0, 0, slice(virtuals // 2, virtuals), n)
        for n in range(tiles // 2):
            p11[:, pair_of_tiles(n, virtuals)] = product(u, w, 1, 1, slice(0, virtuals), n)
            for v in range(n, nv, tiles // 2):
                for t in range(tiles):
                    triangles.place(v, t, True)
        largest[...] = half.largest

    return kernel


def same_kernel(cols):
    def kernel(index, out, p00, p00_rest, p11, largest, kept, sent, _):
        virtuals = p11.shape[0]
        half = Half(out, 0, cols)
        half.largest = largest[...]
        triangles = Triangles(half, p00, p00_rest, p11, virtuals)
        for v in range(virtuals // cols):
            for t in range(lane_tiles(virtuals)):
                triangles.place(v, t, False)
        half.finish(index, kept, sent)

    return kernel


def on_chip(body, name, out_shape, scratch, flops, index, u, w, *arrays):
    results = pl.pallas_call(
        body,
        in_specs=[SMEM] + [VMEM] * (2 + len(arrays)),
        out_specs=[VMEM] * len(out_shape),
        out_shape=out_shape,
        scratch_shapes=[pltpu.VMEM(shape, F32) for shape in scratch],
        name=name,
        cost_estimate=pl.CostEstimate(flops=flops, bytes_accessed=2**20, transcendentals=0),
        compiler_params=pltpu.CompilerParams(vmem_limit_bytes=3 * 2**20),
    )(index, u, w, *arrays)
    return results, u, w


def crossed_sums(index, amplitudes, integrals, half_types, cols):
    _, depth, virtuals, inner = amplitudes.shape
    tiles = lane_tiles(virtuals)
    width, nv = half_types[0].shape[-1], virtuals // cols
    kept, sent, u, w = pl.pallas_call(
        crossed_kernel(cols),
        in_specs=[SMEM, ANY, ANY],
        out_specs=[VMEM] * 4,
        out_shape=[
            *half_types,
            jax.ShapeDtypeStruct(amplitudes.shape, BF16),
            jax.ShapeDtypeStruct((tiles * depth * inner * 2, LANES), BF16),
        ],
        scratch_shapes=[
            pltpu.VMEM((virtuals, virtuals), F32),
            pltpu.VMEM((virtuals, 4 * LANES), F32),
            pltpu.VMEM((nv, virtuals, width), F32),
            pltpu.VMEM((min(5, depth), 2 * inner, virtuals), BF16),
            pltpu.SemaphoreType.DMA((2, depth)),
            pltpu.SemaphoreType.DMA((depth,)),
        ],
        name="crossed",
        cost_estimate=pl.CostEstimate(
            flops=4 * depth * inner * virtuals * virtuals, bytes_accessed=4 * amplitudes.size, transcendentals=0
        ),
        compiler_params=pltpu.CompilerParams(vmem_limit_bytes=18 * 2**20),
    )(index, amplitudes, integrals)
    return (kept, sent), u, w


def after(value, *others):
    return lax.optimization_barrier((value, *others))[0]


def plain_sums(index, amplitudes, integrals, same, nv, width):
    virtuals = amplitudes.shape[2]
    cols = virtuals // nv

    def cycle(i, j):
        return jnp.einsum("kac,kcb->ab", amplitudes[i], integrals[:, :, j], preferred_element_type=F32)

    if same:
        s00, s11 = ((q + q.T) for q in (cycle(0, 0), cycle(1, 1)))
        a, b = (iota((virtuals, virtuals), axis) for axis in range(2))
        block, diagonal = jnp.where(a <= b, s00, s11), jnp.diagonal(s11)
    else:
        block, diagonal = cycle(0, 1) + cycle(1, 0).T, jnp.zeros((virtuals,), F32)
    largest = jnp.maximum(jnp.max(jnp.abs(block)), jnp.max(jnp.abs(diagonal)))
    parts = block.reshape(virtuals, nv, cols).transpose(1, 0, 2)
    extra = jnp.stack([diagonal, jnp.full((virtuals,), largest)], axis=1)
    extra = jnp.pad(extra, ((0, 0), (0, width - cols - 2)))
    parts = jnp.concatenate([parts, jnp.broadcast_to(extra, (nv, *extra.shape))], axis=2)
    parts = parts.reshape(nv // 2, 2, virtuals, width)
    return [lax.dynamic_index_in_dim(parts, c, 1, keepdims=False) for c in (index[1], 1 - index[1])]


def solution(mesh):
    np_, nv = mesh.shape["pair"], mesh.shape["virt"]
    nx, nz, ratio = nv // 2, np_ // 2, np_ // nv

    def send(block, move):
        pairs = []
        for p in range(np_):
            for v in range(nv):
                q, w = move(p, v)
                pairs.append((p * nv + v, q * nv + w))
        return lax.ppermute(block, AXES, pairs)

    def shards(amplitudes, integrals):
        _, _, virtuals, inner = amplitudes.shape
        rows, cols = virtuals // np_, virtuals // nv
        width = -(-(cols + 2) // LANES) * LANES
        at = cols + 1
        aligned = rows % 8 == 0 and inner % 16 == 0 and virtuals % 64 == 0
        p, v = lax.axis_index("pair"), lax.axis_index("virt")
        index = jnp.stack([v // 2, v % 2, p // 2, p % 2, p, v]).astype(jnp.int32)
        steps = [(dx, dy) for dx in range(nx - 1, -1, -1) for dy in (1, 0) if dx or dy]

        def chip_sum(index, kept, came):
            x, y = index[0], index[3]
            bound = sent_bound(bound_at(kept[0, 0, 0], at) + bound_at(came[0, 0, 0], at))

            def block(x_at, y_at, z):
                return kept[x_at, z, y_at] + came[x_at, z, y_at]

            own = [block(x, y, z) for z in range(nz)]
            results = [[with_bound(own[0], bound, at)] + own[1:]]
            for dx, dy in steps:
                blocks = [coded(block((x + dx) % nx, (y + dy) % 2, z), bound) for z in range(nz)]
                results.append([with_bound(blocks[0], bound, at)] + blocks[1:])
            return results

        def plane_sum(index, own, *came):
            z_own = index[2]
            bounds = [bound_at(array[0], at) for array in came]
            bound = sent_bound(sum(bounds, bound_at(own[0], at)))

            def block(z):
                total = own[z]
                for array, of in zip(came, bounds):
                    total = total + decoded(array[z], of)
                return total

            results = [with_bound(block(z_own), bound, at)]
            for dz in range(1, nz):
                results.append(with_bound(coded(block((z_own + dz) % nz), bound), bound, at))
            return results

        tile_width = -(-(rows + 1) // LANES) * LANES

        def line_sum(count, paired):
            def body(index, own, *arrays):
                total = own[...]
                bound = bound_at(total, at)
                for array in arrays[:count]:
                    array = array[...]
                    total = total + decoded(array, bound_at(array, at))
                    bound = bound + bound_at(array, at)
                bound = sent_bound(bound)
                flipped = [total[:, h * rows : (h + 1) * rows].T for h in range(ratio)]
                results = [total]
                for t in range(ratio):
                    tile = flipped[0]
                    for h in range(1, ratio):
                        tile = jnp.where((index[4] + t) % ratio == h, flipped[h], tile)
                    tile = coded(tile, bound)
                    tile = jnp.concatenate([tile, jnp.broadcast_to(bound, (rows, tile_width - rows))], axis=1)
                    results.append([arrays[count + t][...], tile] if paired else tile)
                return results

            return body

        def outcome(index, crossed, same, *came):
            def mirrored(which):
                parts = []
                for h in range(ratio):
                    part = came[0][which].astype(F32)
                    for t in range(1, ratio):
                        part = jnp.where((index[4] + ratio - h) % ratio == t, came[t][which].astype(F32), part)
                    parts.append(decoded(part[:, :rows], bound_at(part, rows)))
                return jnp.concatenate(parts, axis=1) if ratio > 1 else parts[0]

            same = same[...]
            square = same[:, :cols]
            other = mirrored(1)
            a = index[4] * rows + iota(square.shape, 0)
            b = index[5] * cols + iota(square.shape, 1)
            out00 = jnp.where(a <= b, square, other)
            out11 = jnp.where(a > b, square, jnp.where(a == b, same[:, cols : cols + 1], other))
            return [out00, crossed[...][:, :cols], mirrored(0), out11]

        def outcome_kernel(index, *refs):
            for n, block in enumerate(outcome(index, *refs[:-1])):
                refs[-1][n // 2, :, n % 2, :] = block

        def kind(shape, dtype=F32):
            return jax.ShapeDtypeStruct(shape, dtype)

        work = amplitudes.size * virtuals

        def across_core(pair_of):
            return pair_of[0], send(pair_of[1], lambda p, v: (p, v ^ 1))

        def across_plane(index, kept, came):
            shape = (nx, nz, 2, rows, width)
            types = [kind((nz, rows, width))] + [kind((nz, rows, width), BF16)] * len(steps)
            own, *outs = local(chip_sum, types, aligned, "chip_sum", work)(index, kept.reshape(shape), came.reshape(shape))
            came = [send(block, lambda p, v: (p ^ dy, (v + 2 * dx) % nv)) for (dx, dy), block in zip(steps, outs)]
            return own, came

        def across_line(index, own, came):
            types = [kind((rows, width))] + [kind((rows, width), BF16)] * (nz - 1)
            own, *outs = local(plane_sum, types, aligned, "plane_sum", 2 * work)(index, own, *came)
            return own, [send(block, lambda p, v: ((p + 2 * dz) % np_, v)) for dz, block in zip(range(1, nz), outs)]

        def line_total(index, own, came, first_tiles=()):
            shape = (2, rows, tile_width) if first_tiles else (rows, tile_width)
            types = [kind((rows, width))] + [kind(shape, BF16)] * ratio
            body = line_sum(len(came), bool(first_tiles))
            return local(body, types, aligned, "line_sum")(index, own, *came, *first_tiles)

        def exchanged(tiles):
            return [
                send(tile, lambda p, v: (ratio * v + (p % ratio + t) % ratio, p // ratio)) for t, tile in enumerate(tiles)
            ]

        if aligned:
            half_types = [kind((nx, virtuals, width))] * 2
            crossed, u, w = crossed_sums(index, amplitudes, integrals, half_types, cols)
            crossed = across_core(crossed)
            square = kind((virtuals // 2, virtuals))
            (p00,), u, w = on_chip(
                first_square_kernel, "first_square", [square], [], work // 2, after(index, crossed[0]), u, w
            )
            crossed = across_plane(after(index, p00), *crossed)
            placed = kind((nv, virtuals, width))
            (p00_rest, p11, out, largest), u, w = on_chip(
                other_squares_kernel(cols),
                "other_squares",
                [square, kind((virtuals, virtuals)), placed, kind((1, cols))],
                [],
                3 * work // 2,
                after(index, crossed[0]),
                u,
                w,
                p00,
            )
            *same, _ = pl.pallas_call(
                same_kernel(cols),
                in_specs=[SMEM] + [VMEM] * 5,
                out_specs=[VMEM] * 3,
                out_shape=[*half_types, placed],
                input_output_aliases={1: 2},
                name="same",
                cost_estimate=pl.CostEstimate(flops=work // 2, bytes_accessed=2**20, transcendentals=0),
                compiler_params=pltpu.CompilerParams(vmem_limit_bytes=3 * 2**20),
            )(after(index, p11, *crossed[1]), out, p00, p00_rest, p11, largest)
            crossed = across_line(after(index, same[0]), *crossed)
            same = across_core(same)
            same = across_plane(after(index, crossed[0]), *same)
            crossed, *tiles = line_total(after(index, same[0]), *crossed)
            same = across_line(after(index, crossed), *same)
        else:
            crossed, same = (
                across_line(index, *across_plane(index, *across_core(plain_sums(index, amplitudes, integrals, kind_same, nv, width))))
                for kind_same in (False, True)
            )
            crossed, *tiles = line_total(index, *crossed)
        same, *tiles = line_total(index, *same, tiles)
        arrays = [crossed, same, *exchanged(tiles)]
        if not aligned:
            blocks = outcome(index, *arrays)
            return jnp.stack([jnp.stack(blocks[:2], 1), jnp.stack(blocks[2:], 1)])
        return pl.pallas_call(
            outcome_kernel,
            in_specs=[SMEM] + [VMEM] * len(arrays),
            out_specs=VMEM,
            out_shape=kind((2, rows, 2, cols)),
            name="outcome",
            compiler_params=pltpu.CompilerParams(vmem_limit_bytes=8 * 2**20),
        )(index, *arrays)

    placed = (P(None, "pair", None, "virt"), P("pair", "virt", None, None))
    return jax.shard_map(
        shards, mesh=mesh, in_specs=placed, out_specs=P(None, "pair", None, "virt"), check_vma=False
    )
```

```python
import math

import jax
import jax.numpy as jnp
from jax import lax
from jax.experimental import pallas as pl
from jax.experimental.pallas import tpu as pltpu
from jax.sharding import PartitionSpec as P

AXES = ("pair", "virt")
F32, BF16 = jnp.float32, jnp.bfloat16
TOP = 1024.0
LANES = 128
ANY = pl.BlockSpec(memory_space=pl.ANY)
VMEM = pl.BlockSpec(memory_space=pltpu.VMEM)
SMEM = pl.BlockSpec(memory_space=pltpu.SMEM)


def dot(left, right):
    return jnp.dot(left, right, preferred_element_type=F32)


def iota(shape, axis):
    return lax.broadcasted_iota(jnp.int32, shape, axis)


def bound_at(block, at):
    return block[0:1, at : at + 1].astype(F32)


def with_bound(block, bound, at):
    here = (iota(block.shape, 0) == 0) & (iota(block.shape, 1) == at)
    return jnp.where(here, bound, block)


def sent_bound(bound):
    return jnp.maximum(bound * 1.01, 1e-35).astype(BF16).astype(F32)


def coded(values, bound):
    scaled = jnp.abs(values) * (TOP / bound)
    fourth = scaled * scaled
    fourth = fourth * fourth
    power = fourth * fourth * fourth
    return jnp.where(values < 0, -power, power)


def decoded(block, bound):
    power = block.astype(F32)
    magnitude = jnp.exp2(jnp.log2(jnp.maximum(jnp.abs(power), 1e-37)) * (1 / 12)) * (bound * (1 / TOP))
    return jnp.where(power == 0, 0.0, jnp.where(power < 0, -magnitude, magnitude))


def local(body, out_types, aligned, name, cost=0):
    def kernel(index, *refs):
        results = body(index, *refs[: -len(out_types)])
        for ref, result in zip(refs[-len(out_types) :], results):
            if isinstance(result, list):
                for n, block in enumerate(result):
                    ref[n] = block.astype(ref.dtype)
            else:
                ref[...] = result.astype(ref.dtype)

    def call(index, *arrays):
        if not aligned:
            results = body(index, *arrays)
            results = [jnp.stack(result) if isinstance(result, list) else result for result in results]
            return [result.astype(kind.dtype) for result, kind in zip(results, out_types)]
        return pl.pallas_call(
            kernel,
            in_specs=[SMEM] + [VMEM] * len(arrays),
            out_specs=[VMEM] * len(out_types),
            out_shape=out_types,
            name=name,
            cost_estimate=pl.CostEstimate(flops=cost, bytes_accessed=2**20, transcendentals=0),
            compiler_params=pltpu.CompilerParams(vmem_limit_bytes=2 * 2**20),
        )(index, *arrays)

    return call


def lane_tiles(virtuals):
    return -(-virtuals // LANES)


def lanes(tile, virtuals):
    return min(LANES, virtuals - LANES * tile)


def product(u, w, i, j, rows, n, ks=None):
    _, depth, virtuals, inner = u.shape
    total = None
    for k in ks or range(depth):
        parts = [
            w[pl.ds((t * depth + k) * 2 * inner + j, inner, 2), :][:, : lanes(t, virtuals)]
            for t in (2 * n, 2 * n + 1)
        ]
        term = dot(u[i, k, rows, :], jnp.concatenate(parts, axis=1))
        total = term if total is None else total + term
    return total


def pair_of_tiles(n, virtuals):
    return slice(2 * LANES * n, min(2 * LANES * (n + 1), virtuals))


class Half:
    def __init__(self, out, low, cols):
        self.out, self.low, self.cols = out, low, cols
        self.high = low + out.shape[1]
        self.largest = jnp.zeros((1, cols), F32)

    def place(self, v, r0, r1, block):
        self.out[v, r0 - self.low : r1 - self.low, : self.cols] = block
        self.largest = jnp.maximum(self.largest, jnp.max(jnp.abs(block), axis=0, keepdims=True))

    def finish(self, index, kept, sent):
        out, cols = self.out, self.cols
        largest = jnp.max(self.largest)
        for v in range(2):
            head = out[v, 0:8, cols:]
            here = (iota(head.shape, 0) == 0) & (iota(head.shape, 1) == 1)
            out[v, 0:8, cols:] = jnp.where(here, largest, head)
        for core in range(2):

            @pl.when(index[1] == core)
            def _():
                for x in range(kept.shape[0]):
                    kept[x] = out[2 * x + core]
                    sent[x] = out[2 * x + 1 - core]


def crossed_kernel(cols):
    def kernel(index, u_hbm, w_hbm, kept, sent, u, w, other, own, out, ring, u_sems, w_sems):
        _, depth, virtuals, inner = u.shape
        tiles, slots = lane_tiles(virtuals), ring.shape[0]
        everything, pairs = slice(0, virtuals), tiles // 2
        half = Half(out, 0, cols)

        def u_copy(i, k):
            return pltpu.make_async_copy(u_hbm.at[i, k], u.at[i, k], u_sems.at[i, k])

        def w_copy(k):
            source = w_hbm.at[k].reshape(2 * inner, virtuals)
            return pltpu.make_async_copy(source, ring.at[k % slots], w_sems.at[k])

        def take(k):
            w_copy(k).wait()
            for t in range(tiles):
                rows = slice((t * depth + k) * 2 * inner, (t * depth + k + 1) * 2 * inner)
                width = lanes(t, virtuals)
                w[rows, :width] = ring[k % slots, :, LANES * t : LANES * t + width]
            if k + slots < depth:
                w_copy(k + slots).start()

        cuts = [0, 2 * depth // 7, 9 * depth // 14, depth]
        parts = [range(*cuts[n : n + 2]) for n in range(3)]
        for k in range(slots):
            w_copy(k).start()
        for k in parts[0]:
            u_copy(1, k).start()
        for number, ks in enumerate(parts):
            for k in ks:
                take(k)
            for k in ks:
                u_copy(1, k).wait()
            for k in parts[number + 1] if number < 2 else range(depth):
                u_copy(1 if number < 2 else 0, k).start()
            for n in range(pairs):
                term = product(u, w, 1, 0, everything, n, ks)
                columns = pair_of_tiles(n, virtuals)
                other[:, columns] = term if number == 0 else other[:, columns] + term
        for k in range(depth):
            u_copy(0, k).wait()
        v, wide = 0, 2 * LANES
        for n in range(pairs):
            columns = pair_of_tiles(n, virtuals)
            if n:
                own[:, :wide] = own[:, wide:]
            own[:, wide : wide + columns.stop - columns.start] = product(u, w, 0, 1, everything, n)
            while (v + 1) * cols <= columns.stop:
                on, past = v * cols, (v + 1) * cols
                shift = wide - columns.start
                for t in range(tiles):
                    r0, r1 = LANES * t, LANES * t + lanes(t, virtuals)
                    half.place(v, r0, r1, own[r0:r1, on + shift : past + shift] + other[on:past, r0:r1].T)
                v += 1
        half.finish(index, kept, sent)

    return kernel


def first_square_kernel(index, u, w, square):
    virtuals = u.shape[2]
    for n in range(lane_tiles(virtuals) // 2):
        square[:, pair_of_tiles(n, virtuals)] = product(u, w, 0, 0, slice(0, virtuals // 2), n)


class Triangles:
    def __init__(self, half, p00, p00_rest, p11, virtuals):
        self.half, self.p00, self.p00_rest, self.p11, self.virtuals = half, p00, p00_rest, p11, virtuals

    def rows_of(self, i, r0, r1, c0, c1):
        middle = self.virtuals // 2
        if i == 1:
            return self.p11[r0:r1, c0:c1]
        if r1 <= middle:
            return self.p00[r0:r1, c0:c1]
        if r0 >= middle:
            return self.p00_rest[r0 - middle : r1 - middle, c0:c1]
        return jnp.concatenate([self.p00[r0:middle, c0:c1], self.p00_rest[0 : r1 - middle, c0:c1]], axis=0)

    def ready(self, v, tile):
        return max(-(-(v + 1) * self.half.cols // (2 * LANES)) - 1, tile // 2)

    def place(self, v, tile, above):
        half, cols = self.half, self.half.cols
        begin, end = LANES * tile, LANES * tile + lanes(tile, self.virtuals)
        on, past = v * cols, (v + 1) * cols
        flips = {}

        def symmetric(i, r0, r1):
            if i not in flips:
                flips[i] = self.rows_of(i, on, past, begin, end).T
            return self.rows_of(i, r0, r1, on, past) + flips[i][r0 - begin : r1 - begin]

        r0, r1 = begin, min(end, on)
        if above and r0 < r1:
            half.place(v, r0, r1, symmetric(0, r0, r1))
        r0, r1 = max(begin, on), min(end, past)
        if not above and r0 < r1:
            s00, s11 = symmetric(0, r0, r1), symmetric(1, r0, r1)
            a, b = r0 + iota(s00.shape, 0), on + iota(s00.shape, 1)
            half.place(v, r0, r1, jnp.where(a <= b, s00, s11))
            diagonal = jnp.where(a == b, s11, 0.0)
            half.out[v, r0:r1, cols : cols + 1] = jnp.sum(diagonal, axis=1, keepdims=True)
            half.largest = jnp.maximum(half.largest, jnp.max(jnp.abs(diagonal), axis=0, keepdims=True))
        r0, r1 = max(begin, past), end
        if not above and r0 < r1:
            half.place(v, r0, r1, symmetric(1, r0, r1))


def other_squares_kernel(cols):
    def kernel(index, u, w, p00, p00_rest, p11, out, largest):
        virtuals = u.shape[2]
        tiles, nv = lane_tiles(virtuals), virtuals // cols
        half = Half(out, 0, cols)
        triangles = Triangles(half, p00, p00_rest, p11, virtuals)
        for n in range(tiles // 2):
            p00_rest[:, pair_of_tiles(n, virtuals)] = product(u, w, 0, 0, slice(virtuals // 2, virtuals), n)
        for n in range(tiles // 2):
            p11[:, pair_of_tiles(n, virtuals)] = product(u, w, 1, 1, slice(0, virtuals), n)
            for v in range(n, nv, tiles // 2):
                for t in range(tiles):
                    triangles.place(v, t, True)
            for v in range(nv):
                for t in range(tiles):
                    if n == triangles.ready(v, t) < tiles // 2 - 1:
                        triangles.place(v, t, False)
        largest[...] = half.largest

    return kernel


def same_kernel(cols):
    def kernel(index, out, p00, p00_rest, p11, largest, kept, sent, _):
        virtuals = p11.shape[0]
        half = Half(out, 0, cols)
        half.largest = largest[...]
        triangles = Triangles(half, p00, p00_rest, p11, virtuals)
        tiles = lane_tiles(virtuals)
        for v in range(virtuals // cols):
            for t in range(tiles):
                if triangles.ready(v, t) == tiles // 2 - 1:
                    triangles.place(v, t, False)
        half.finish(index, kept, sent)

    return kernel


def on_chip(body, name, out_shape, scratch, flops, index, u, w, *arrays):
    results = pl.pallas_call(
        body,
        in_specs=[SMEM] + [VMEM] * (2 + len(arrays)),
        out_specs=[VMEM] * len(out_shape),
        out_shape=out_shape,
        scratch_shapes=[pltpu.VMEM(shape, F32) for shape in scratch],
        name=name,
        cost_estimate=pl.CostEstimate(flops=flops, bytes_accessed=2**20, transcendentals=0),
        compiler_params=pltpu.CompilerParams(vmem_limit_bytes=3 * 2**20),
    )(index, u, w, *arrays)
    return results, u, w


def crossed_sums(index, amplitudes, integrals, half_types, cols):
    _, depth, virtuals, inner = amplitudes.shape
    tiles = lane_tiles(virtuals)
    width, nv = half_types[0].shape[-1], virtuals // cols
    kept, sent, u, w = pl.pallas_call(
        crossed_kernel(cols),
        in_specs=[SMEM, ANY, ANY],
        out_specs=[VMEM] * 4,
        out_shape=[
            *half_types,
            jax.ShapeDtypeStruct(amplitudes.shape, BF16),
            jax.ShapeDtypeStruct((tiles * depth * inner * 2, LANES), BF16),
        ],
        scratch_shapes=[
            pltpu.VMEM((virtuals, virtuals), F32),
            pltpu.VMEM((virtuals, 4 * LANES), F32),
            pltpu.VMEM((nv, virtuals, width), F32),
            pltpu.VMEM((min(5, depth), 2 * inner, virtuals), BF16),
            pltpu.SemaphoreType.DMA((2, depth)),
            pltpu.SemaphoreType.DMA((depth,)),
        ],
        name="crossed",
        cost_estimate=pl.CostEstimate(
            flops=4 * depth * inner * virtuals * virtuals, bytes_accessed=4 * amplitudes.size, transcendentals=0
        ),
        compiler_params=pltpu.CompilerParams(vmem_limit_bytes=18 * 2**20),
    )(index, amplitudes, integrals)
    return (kept, sent), u, w


def after(value, *others):
    return lax.optimization_barrier((value, *others))[0]


def plain_sums(index, amplitudes, integrals, same, nv, width):
    virtuals = amplitudes.shape[2]
    cols = virtuals // nv

    def cycle(i, j):
        return jnp.einsum("kac,kcb->ab", amplitudes[i], integrals[:, :, j], preferred_element_type=F32)

    if same:
        s00, s11 = ((q + q.T) for q in (cycle(0, 0), cycle(1, 1)))
        a, b = (iota((virtuals, virtuals), axis) for axis in range(2))
        block, diagonal = jnp.where(a <= b, s00, s11), jnp.diagonal(s11)
    else:
        block, diagonal = cycle(0, 1) + cycle(1, 0).T, jnp.zeros((virtuals,), F32)
    largest = jnp.maximum(jnp.max(jnp.abs(block)), jnp.max(jnp.abs(diagonal)))
    parts = block.reshape(virtuals, nv, cols).transpose(1, 0, 2)
    extra = jnp.stack([diagonal, jnp.full((virtuals,), largest)], axis=1)
    extra = jnp.pad(extra, ((0, 0), (0, width - cols - 2)))
    parts = jnp.concatenate([parts, jnp.broadcast_to(extra, (nv, *extra.shape))], axis=2)
    parts = parts.reshape(nv // 2, 2, virtuals, width)
    return [lax.dynamic_index_in_dim(parts, c, 1, keepdims=False) for c in (index[1], 1 - index[1])]


def solution(mesh):
    np_, nv = mesh.shape["pair"], mesh.shape["virt"]
    nx, nz, ratio = nv // 2, np_ // 2, np_ // nv

    def send(block, move):
        pairs = []
        for p in range(np_):
            for v in range(nv):
                q, w = move(p, v)
                pairs.append((p * nv + v, q * nv + w))
        return lax.ppermute(block, AXES, pairs)

    def shards(amplitudes, integrals):
        _, _, virtuals, inner = amplitudes.shape
        rows, cols = virtuals // np_, virtuals // nv
        width = -(-(cols + 2) // LANES) * LANES
        at = cols + 1
        aligned = rows % 8 == 0 and inner % 16 == 0 and virtuals % 64 == 0
        p, v = lax.axis_index("pair"), lax.axis_index("virt")
        index = jnp.stack([v // 2, v % 2, p // 2, p % 2, p, v]).astype(jnp.int32)
        steps = [(dx, dy) for dx in range(nx - 1, -1, -1) for dy in (1, 0) if dx or dy]

        def chip_sum(index, kept, came):
            x, y = index[0], index[3]
            bound = sent_bound(bound_at(kept[0, 0, 0], at) + bound_at(came[0, 0, 0], at))

            def block(x_at, y_at, z):
                return kept[x_at, z, y_at] + came[x_at, z, y_at]

            own = [block(x, y, z) for z in range(nz)]
            results = [[with_bound(own[0], bound, at)] + own[1:]]
            for dx, dy in steps:
                blocks = [coded(block((x + dx) % nx, (y + dy) % 2, z), bound) for z in range(nz)]
                results.append([with_bound(blocks[0], bound, at)] + blocks[1:])
            return results

        def plane_sum(index, own, *came):
            z_own = index[2]
            bounds = [bound_at(array[0], at) for array in came]
            bound = sent_bound(sum(bounds, bound_at(own[0], at)))

            def block(z):
                total = own[z]
                for array, of in zip(came, bounds):
                    total = total + decoded(array[z], of)
                return total

            results = [with_bound(block(z_own), bound, at)]
            for dz in range(1, nz):
                results.append(with_bound(coded(block(z_own ^ dz), bound), bound, at))
            return results

        tile_width = -(-(rows + 1) // LANES) * LANES

        def line_sum(count, paired):
            def body(index, own, *arrays):
                total = own[...]
                bound = bound_at(total, at)
                for array in arrays[:count]:
                    array = array[...]
                    total = total + decoded(array, bound_at(array, at))
                    bound = bound + bound_at(array, at)
                bound = sent_bound(bound)
                flipped = [total[:, h * rows : (h + 1) * rows].T for h in range(ratio)]
                results = [total]
                for t in range(ratio):
                    tile = flipped[0]
                    for h in range(1, ratio):
                        tile = jnp.where((index[4] + t) % ratio == h, flipped[h], tile)
                    tile = coded(tile, bound)
                    tile = jnp.concatenate([tile, jnp.broadcast_to(bound, (rows, tile_width - rows))], axis=1)
                    results.append([arrays[count + t][...], tile] if paired else tile)
                return results

            return body

        def outcome(index, crossed, same, *came):
            def mirrored(which):
                parts = []
                for h in range(ratio):
                    part = came[0][which].astype(F32)
                    for t in range(1, ratio):
                        part = jnp.where((index[4] + ratio - h) % ratio == t, came[t][which].astype(F32), part)
                    parts.append(decoded(part[:, :rows], bound_at(part, rows)))
                return jnp.concatenate(parts, axis=1) if ratio > 1 else parts[0]

            same = same[...]
            square = same[:, :cols]
            other = mirrored(1)
            a = index[4] * rows + iota(square.shape, 0)
            b = index[5] * cols + iota(square.shape, 1)
            out00 = jnp.where(a <= b, square, other)
            out11 = jnp.where(a > b, square, jnp.where(a == b, same[:, cols : cols + 1], other))
            return [out00, crossed[...][:, :cols], mirrored(0), out11]

        def outcome_kernel(index, *refs):
            for n, block in enumerate(outcome(index, *refs[:-1])):
                refs[-1][n // 2, :, n % 2, :] = block

        def kind(shape, dtype=F32):
            return jax.ShapeDtypeStruct(shape, dtype)

        work = amplitudes.size * virtuals

        def across_core(pair_of):
            return pair_of[0], send(pair_of[1], lambda p, v: (p, v ^ 1))

        def across_plane(index, kept, came):
            shape = (nx, nz, 2, rows, width)
            types = [kind((nz, rows, width))] + [kind((nz, rows, width), BF16)] * len(steps)
            own, *outs = local(chip_sum, types, aligned, "chip_sum", work)(index, kept.reshape(shape), came.reshape(shape))
            came = [send(block, lambda p, v: (p ^ dy, (v + 2 * dx) % nv)) for (dx, dy), block in zip(steps, outs)]
            return own, came

        def across_line(index, own, came):
            types = [kind((rows, width))] + [kind((rows, width), BF16)] * (nz - 1)
            own, *outs = local(plane_sum, types, aligned, "plane_sum", 2 * work)(index, own, *came)
            return own, [send(block, lambda p, v: (p ^ 2 * dz, v)) for dz, block in zip(range(1, nz), outs)]

        def line_total(index, own, came, first_tiles=()):
            shape = (2, rows, tile_width) if first_tiles else (rows, tile_width)
            types = [kind((rows, width))] + [kind(shape, BF16)] * ratio
            body = line_sum(len(came), bool(first_tiles))
            return local(body, types, aligned, "line_sum")(index, own, *came, *first_tiles)

        def exchanged(tiles):
            return [
                send(tile, lambda p, v: (ratio * v + (p % ratio + t) % ratio, p // ratio)) for t, tile in enumerate(tiles)
            ]

        if aligned:
            half_types = [kind((nx, virtuals, width))] * 2
            crossed, u, w = crossed_sums(index, amplitudes, integrals, half_types, cols)
            crossed = across_core(crossed)
            square = kind((virtuals // 2, virtuals))
            (p00,), u, w = on_chip(
                first_square_kernel, "first_square", [square], [], work // 2, after(index, crossed[0]), u, w
            )
            crossed = across_plane(after(index, p00), *crossed)
            placed = kind((nv, virtuals, width))
            (p00_rest, p11, out, largest), u, w = on_chip(
                other_squares_kernel(cols),
                "other_squares",
                [square, kind((virtuals, virtuals)), placed, kind((1, cols))],
                [],
                3 * work // 2,
                after(index, crossed[0]),
                u,
                w,
                p00,
            )
            *same, _ = pl.pallas_call(
                same_kernel(cols),
                in_specs=[SMEM] + [VMEM] * 5,
                out_specs=[VMEM] * 3,
                out_shape=[*half_types, placed],
                input_output_aliases={1: 2},
                name="same",
                cost_estimate=pl.CostEstimate(flops=work // 2, bytes_accessed=2**20, transcendentals=0),
                compiler_params=pltpu.CompilerParams(vmem_limit_bytes=3 * 2**20),
            )(after(index, p11, *crossed[1]), out, p00, p00_rest, p11, largest)
            crossed = across_line(after(index, same[0]), *crossed)
            same = across_core(same)
            same = across_plane(after(index, crossed[0]), *same)
            crossed, *tiles = line_total(after(index, same[0]), *crossed)
            same = across_line(after(index, crossed), *same)
        else:
            crossed, same = (
                across_line(index, *across_plane(index, *across_core(plain_sums(index, amplitudes, integrals, kind_same, nv, width))))
                for kind_same in (False, True)
            )
            crossed, *tiles = line_total(index, *crossed)
        same, *tiles = line_total(index, *same, tiles)
        arrays = [crossed, same, *exchanged(tiles)]
        if not aligned:
            blocks = outcome(index, *arrays)
            return jnp.stack([jnp.stack(blocks[:2], 1), jnp.stack(blocks[2:], 1)])
        return pl.pallas_call(
            outcome_kernel,
            in_specs=[SMEM] + [VMEM] * len(arrays),
            out_specs=VMEM,
            out_shape=kind((2, rows, 2, cols)),
            name="outcome",
            compiler_params=pltpu.CompilerParams(vmem_limit_bytes=8 * 2**20),
        )(index, *arrays)

    placed = (P(None, "pair", None, "virt"), P("pair", "virt", None, None))
    return jax.shard_map(
        shards, mesh=mesh, in_specs=placed, out_specs=P(None, "pair", None, "virt"), check_vma=False
    )
```

```python
import math

import jax
import jax.numpy as jnp
from jax import lax
from jax.experimental import pallas as pl
from jax.experimental.pallas import tpu as pltpu
from jax.sharding import PartitionSpec as P

AXES = ("pair", "virt")
F32, BF16 = jnp.float32, jnp.bfloat16
TOP = 1024.0
LANES = 128
ANY = pl.BlockSpec(memory_space=pl.ANY)
VMEM = pl.BlockSpec(memory_space=pltpu.VMEM)
SMEM = pl.BlockSpec(memory_space=pltpu.SMEM)


def dot(left, right):
    return jnp.dot(left, right, preferred_element_type=F32)


def iota(shape, axis):
    return lax.broadcasted_iota(jnp.int32, shape, axis)


def bound_at(block, at):
    return block[0:1, at : at + 1].astype(F32)


def with_bound(block, bound, at):
    here = (iota(block.shape, 0) == 0) & (iota(block.shape, 1) == at)
    return jnp.where(here, bound, block)


def sent_bound(bound, index):
    more = ((5 * index[4] + 11 * index[5]) % 16).astype(F32)
    return jnp.maximum(bound * (1.01 + 0.0037 * more), 1e-35).astype(BF16).astype(F32)


def coded(values, bound):
    scaled = jnp.abs(values) * (TOP / bound)
    fourth = scaled * scaled
    fourth = fourth * fourth
    power = fourth * fourth * fourth
    return jnp.where(values < 0, -power, power)


def decoded(block, bound):
    power = block.astype(F32)
    magnitude = jnp.exp2(jnp.log2(jnp.maximum(jnp.abs(power), 1e-37)) * (1 / 12)) * (bound * (1 / TOP))
    return jnp.where(power == 0, 0.0, jnp.where(power < 0, -magnitude, magnitude))


def local(body, out_types, aligned, name, cost=0):
    def kernel(index, *refs):
        results = body(index, *refs[: -len(out_types)])
        for ref, result in zip(refs[-len(out_types) :], results):
            if isinstance(result, list):
                for n, block in enumerate(result):
                    ref[n] = block.astype(ref.dtype)
            else:
                ref[...] = result.astype(ref.dtype)

    def call(index, *arrays):
        if not aligned:
            results = body(index, *arrays)
            results = [jnp.stack(result) if isinstance(result, list) else result for result in results]
            return [result.astype(kind.dtype) for result, kind in zip(results, out_types)]
        return pl.pallas_call(
            kernel,
            in_specs=[SMEM] + [VMEM] * len(arrays),
            out_specs=[VMEM] * len(out_types),
            out_shape=out_types,
            name=name,
            cost_estimate=pl.CostEstimate(flops=cost, bytes_accessed=2**20, transcendentals=0),
            compiler_params=pltpu.CompilerParams(vmem_limit_bytes=2 * 2**20),
        )(index, *arrays)

    return call


def lane_tiles(virtuals):
    return -(-virtuals // LANES)


def lanes(tile, virtuals):
    return min(LANES, virtuals - LANES * tile)


def product(u, w, i, j, rows, n, ks=None):
    _, depth, virtuals, inner = u.shape
    total = None
    for k in ks or range(depth):
        parts = [
            w[pl.ds((t * depth + k) * 2 * inner + j, inner, 2), :][:, : lanes(t, virtuals)]
            for t in (2 * n, 2 * n + 1)
        ]
        term = dot(u[i, k, rows, :], jnp.concatenate(parts, axis=1))
        total = term if total is None else total + term
    return total


def pair_of_tiles(n, virtuals):
    return slice(2 * LANES * n, min(2 * LANES * (n + 1), virtuals))


class Half:
    def __init__(self, out, low, cols):
        self.out, self.low, self.cols = out, low, cols
        self.high = low + out.shape[1]
        self.largest = jnp.zeros((1, cols), F32)

    def place(self, v, r0, r1, block):
        self.out[v, r0 - self.low : r1 - self.low, : self.cols] = block
        self.largest = jnp.maximum(self.largest, jnp.max(jnp.abs(block), axis=0, keepdims=True))

    def finish(self, index, kept, sent):
        out, cols = self.out, self.cols
        largest = jnp.max(self.largest)
        for v in range(2):
            head = out[v, 0:8, cols:]
            here = (iota(head.shape, 0) == 0) & (iota(head.shape, 1) == 1)
            out[v, 0:8, cols:] = jnp.where(here, largest, head)
        for core in range(2):

            @pl.when(index[1] == core)
            def _():
                for x in range(kept.shape[0]):
                    kept[x] = out[2 * x + core]
                    sent[x] = out[2 * x + 1 - core]


def crossed_kernel(cols):
    def kernel(index, u_hbm, w_hbm, kept, sent, u, w, other, own, out, ring, u_sems, w_sems):
        _, depth, virtuals, inner = u.shape
        tiles, slots = lane_tiles(virtuals), ring.shape[0]
        everything, pairs = slice(0, virtuals), tiles // 2
        half = Half(out, 0, cols)

        def u_copy(i, k):
            return pltpu.make_async_copy(u_hbm.at[i, k], u.at[i, k], u_sems.at[i, k])

        def w_copy(k):
            source = w_hbm.at[k].reshape(2 * inner, virtuals)
            return pltpu.make_async_copy(source, ring.at[k % slots], w_sems.at[k])

        def take(k):
            w_copy(k).wait()
            for t in range(tiles):
                rows = slice((t * depth + k) * 2 * inner, (t * depth + k + 1) * 2 * inner)
                width = lanes(t, virtuals)
                w[rows, :width] = ring[k % slots, :, LANES * t : LANES * t + width]
            if k + slots < depth:
                w_copy(k + slots).start()

        cuts = [0, 2 * depth // 7, 9 * depth // 14, depth]
        parts = [range(*cuts[n : n + 2]) for n in range(3)]
        for k in range(slots):
            w_copy(k).start()
        for k in parts[0]:
            u_copy(1, k).start()
        for number, ks in enumerate(parts):
            for k in ks:
                take(k)
            for k in ks:
                u_copy(1, k).wait()
            for k in parts[number + 1] if number < 2 else range(depth):
                u_copy(1 if number < 2 else 0, k).start()
            for n in range(pairs):
                term = product(u, w, 1, 0, everything, n, ks)
                columns = pair_of_tiles(n, virtuals)
                other[:, columns] = term if number == 0 else other[:, columns] + term
        for k in range(depth):
            u_copy(0, k).wait()
        v, wide = 0, 2 * LANES
        for n in range(pairs):
            columns = pair_of_tiles(n, virtuals)
            if n:
                own[:, :wide] = own[:, wide:]
            own[:, wide : wide + columns.stop - columns.start] = product(u, w, 0, 1, everything, n)
            while (v + 1) * cols <= columns.stop:
                on, past = v * cols, (v + 1) * cols
                shift = wide - columns.start
                for t in range(tiles):
                    r0, r1 = LANES * t, LANES * t + lanes(t, virtuals)
                    half.place(v, r0, r1, own[r0:r1, on + shift : past + shift] + other[on:past, r0:r1].T)
                v += 1
        half.finish(index, kept, sent)

    return kernel


def first_square_kernel(index, u, w, square):
    virtuals = u.shape[2]
    for n in range(lane_tiles(virtuals) // 2):
        square[:, pair_of_tiles(n, virtuals)] = product(u, w, 0, 0, slice(0, virtuals // 2), n)


class Triangles:
    def __init__(self, half, p00, p00_rest, p11, virtuals):
        self.half, self.p00, self.p00_rest, self.p11, self.virtuals = half, p00, p00_rest, p11, virtuals

    def rows_of(self, i, r0, r1, c0, c1):
        middle = self.virtuals // 2
        if i == 1:
            return self.p11[r0:r1, c0:c1]
        if r1 <= middle:
            return self.p00[r0:r1, c0:c1]
        if r0 >= middle:
            return self.p00_rest[r0 - middle : r1 - middle, c0:c1]
        return jnp.concatenate([self.p00[r0:middle, c0:c1], self.p00_rest[0 : r1 - middle, c0:c1]], axis=0)

    def ready(self, v, tile):
        return max(-(-(v + 1) * self.half.cols // (2 * LANES)) - 1, tile // 2)

    def place(self, v, tile, above):
        half, cols = self.half, self.half.cols
        begin, end = LANES * tile, LANES * tile + lanes(tile, self.virtuals)
        on, past = v * cols, (v + 1) * cols
        flips = {}

        def symmetric(i, r0, r1):
            if i not in flips:
                flips[i] = self.rows_of(i, on, past, begin, end).T
            return self.rows_of(i, r0, r1, on, past) + flips[i][r0 - begin : r1 - begin]

        r0, r1 = begin, min(end, on)
        if above and r0 < r1:
            half.place(v, r0, r1, symmetric(0, r0, r1))
        r0, r1 = max(begin, on), min(end, past)
        if not above and r0 < r1:
            s00, s11 = symmetric(0, r0, r1), symmetric(1, r0, r1)
            a, b = r0 + iota(s00.shape, 0), on + iota(s00.shape, 1)
            half.place(v, r0, r1, jnp.where(a <= b, s00, s11))
            diagonal = jnp.where(a == b, s11, 0.0)
            half.out[v, r0:r1, cols : cols + 1] = jnp.sum(diagonal, axis=1, keepdims=True)
            half.largest = jnp.maximum(half.largest, jnp.max(jnp.abs(diagonal), axis=0, keepdims=True))
        r0, r1 = max(begin, past), end
        if not above and r0 < r1:
            half.place(v, r0, r1, symmetric(1, r0, r1))


def other_squares_kernel(cols):
    def kernel(index, u, w, p00, p00_rest, p11, out, largest):
        virtuals = u.shape[2]
        tiles, nv = lane_tiles(virtuals), virtuals // cols
        half = Half(out, 0, cols)
        triangles = Triangles(half, p00, p00_rest, p11, virtuals)
        for n in range(tiles // 2):
            p00_rest[:, pair_of_tiles(n, virtuals)] = product(u, w, 0, 0, slice(virtuals // 2, virtuals), n)
        for n in range(tiles // 2):
            p11[:, pair_of_tiles(n, virtuals)] = product(u, w, 1, 1, slice(0, virtuals), n)
            for v in range(n, nv, tiles // 2):
                for t in range(tiles):
                    triangles.place(v, t, True)
            for v in range(nv):
                for t in range(tiles):
                    if n == triangles.ready(v, t) < tiles // 2 - 1:
                        triangles.place(v, t, False)
        largest[...] = half.largest

    return kernel


def same_kernel(cols):
    def kernel(index, out, p00, p00_rest, p11, largest, kept, sent, _):
        virtuals = p11.shape[0]
        half = Half(out, 0, cols)
        half.largest = largest[...]
        triangles = Triangles(half, p00, p00_rest, p11, virtuals)
        tiles = lane_tiles(virtuals)
        for v in range(virtuals // cols):
            for t in range(tiles):
                if triangles.ready(v, t) == tiles // 2 - 1:
                    triangles.place(v, t, False)
        half.finish(index, kept, sent)

    return kernel


def on_chip(body, name, out_shape, scratch, flops, index, u, w, *arrays):
    results = pl.pallas_call(
        body,
        in_specs=[SMEM] + [VMEM] * (2 + len(arrays)),
        out_specs=[VMEM] * len(out_shape),
        out_shape=out_shape,
        scratch_shapes=[pltpu.VMEM(shape, F32) for shape in scratch],
        name=name,
        cost_estimate=pl.CostEstimate(flops=flops, bytes_accessed=2**20, transcendentals=0),
        compiler_params=pltpu.CompilerParams(vmem_limit_bytes=3 * 2**20),
    )(index, u, w, *arrays)
    return results, u, w


def crossed_sums(index, amplitudes, integrals, half_types, cols):
    _, depth, virtuals, inner = amplitudes.shape
    tiles = lane_tiles(virtuals)
    width, nv = half_types[0].shape[-1], virtuals // cols
    kept, sent, u, w = pl.pallas_call(
        crossed_kernel(cols),
        in_specs=[SMEM, ANY, ANY],
        out_specs=[VMEM] * 4,
        out_shape=[
            *half_types,
            jax.ShapeDtypeStruct(amplitudes.shape, BF16),
            jax.ShapeDtypeStruct((tiles * depth * inner * 2, LANES), BF16),
        ],
        scratch_shapes=[
            pltpu.VMEM((virtuals, virtuals), F32),
            pltpu.VMEM((virtuals, 4 * LANES), F32),
            pltpu.VMEM((nv, virtuals, width), F32),
            pltpu.VMEM((min(5, depth), 2 * inner, virtuals), BF16),
            pltpu.SemaphoreType.DMA((2, depth)),
            pltpu.SemaphoreType.DMA((depth,)),
        ],
        name="crossed",
        cost_estimate=pl.CostEstimate(
            flops=4 * depth * inner * virtuals * virtuals, bytes_accessed=4 * amplitudes.size, transcendentals=0
        ),
        compiler_params=pltpu.CompilerParams(vmem_limit_bytes=18 * 2**20),
    )(index, amplitudes, integrals)
    return (kept, sent), u, w


def after(value, *others):
    return lax.optimization_barrier((value, *others))[0]


def plain_sums(index, amplitudes, integrals, same, nv, width):
    virtuals = amplitudes.shape[2]
    cols = virtuals // nv

    def cycle(i, j):
        return jnp.einsum("kac,kcb->ab", amplitudes[i], integrals[:, :, j], preferred_element_type=F32)

    if same:
        s00, s11 = ((q + q.T) for q in (cycle(0, 0), cycle(1, 1)))
        a, b = (iota((virtuals, virtuals), axis) for axis in range(2))
        block, diagonal = jnp.where(a <= b, s00, s11), jnp.diagonal(s11)
    else:
        block, diagonal = cycle(0, 1) + cycle(1, 0).T, jnp.zeros((virtuals,), F32)
    largest = jnp.maximum(jnp.max(jnp.abs(block)), jnp.max(jnp.abs(diagonal)))
    parts = block.reshape(virtuals, nv, cols).transpose(1, 0, 2)
    extra = jnp.stack([diagonal, jnp.full((virtuals,), largest)], axis=1)
    extra = jnp.pad(extra, ((0, 0), (0, width - cols - 2)))
    parts = jnp.concatenate([parts, jnp.broadcast_to(extra, (nv, *extra.shape))], axis=2)
    parts = parts.reshape(nv // 2, 2, virtuals, width)
    return [lax.dynamic_index_in_dim(parts, c, 1, keepdims=False) for c in (index[1], 1 - index[1])]


def solution(mesh):
    np_, nv = mesh.shape["pair"], mesh.shape["virt"]
    nx, nz, ratio = nv // 2, np_ // 2, np_ // nv

    def send(block, move):
        pairs = []
        for p in range(np_):
            for v in range(nv):
                q, w = move(p, v)
                pairs.append((p * nv + v, q * nv + w))
        return lax.ppermute(block, AXES, pairs)

    def shards(amplitudes, integrals):
        _, _, virtuals, inner = amplitudes.shape
        rows, cols = virtuals // np_, virtuals // nv
        width = -(-(cols + 2) // LANES) * LANES
        at = cols + 1
        aligned = rows % 8 == 0 and inner % 16 == 0 and virtuals % 64 == 0
        p, v = lax.axis_index("pair"), lax.axis_index("virt")
        index = jnp.stack([v // 2, v % 2, p // 2, p % 2, p, v]).astype(jnp.int32)
        steps = [(dx, dy) for dx in range(nx - 1, -1, -1) for dy in (1, 0) if dx or dy]

        def chip_sum(index, kept, came):
            x, y = index[0], index[3]
            bound = sent_bound(bound_at(kept[0, 0, 0], at) + bound_at(came[0, 0, 0], at), index)

            def block(x_at, y_at, z):
                return kept[x_at, z, y_at] + came[x_at, z, y_at]

            own = [block(x, y, z) for z in range(nz)]
            results = [[with_bound(own[0], bound, at)] + own[1:]]
            for dx, dy in steps:
                blocks = [coded(block((x + dx) % nx, (y + dy) % 2, z), bound) for z in range(nz)]
                results.append([with_bound(blocks[0], bound, at)] + blocks[1:])
            return results

        def plane_sum(index, own, *came):
            z_own = index[2]
            bounds = [bound_at(array[0], at) for array in came]
            bound = sent_bound(sum(bounds, bound_at(own[0], at)), index)

            def block(z):
                total = own[z]
                for array, of in zip(came, bounds):
                    total = total + decoded(array[z], of)
                return total

            results = [with_bound(block(z_own), bound, at)]
            for dz in range(1, nz):
                results.append(with_bound(coded(block(z_own ^ dz), bound), bound, at))
            return results

        tile_width = -(-(rows + 1) // LANES) * LANES

        def line_sum(count, paired):
            def body(index, own, *arrays):
                total = own[...]
                bound = bound_at(total, at)
                for array in arrays[:count]:
                    array = array[...]
                    total = total + decoded(array, bound_at(array, at))
                    bound = bound + bound_at(array, at)
                bound = sent_bound(bound, index)
                flipped = [total[:, h * rows : (h + 1) * rows].T for h in range(ratio)]
                results = [total]
                for t in range(ratio):
                    tile = flipped[0]
                    for h in range(1, ratio):
                        tile = jnp.where((index[4] + t) % ratio == h, flipped[h], tile)
                    tile = coded(tile, bound)
                    tile = jnp.concatenate([tile, jnp.broadcast_to(bound, (rows, tile_width - rows))], axis=1)
                    results.append([arrays[count + t][...], tile] if paired else tile)
                return results

            return body

        def outcome(index, crossed, same, *came):
            def mirrored(which):
                parts = []
                for h in range(ratio):
                    part = came[0][which].astype(F32)
                    for t in range(1, ratio):
                        part = jnp.where((index[4] + ratio - h) % ratio == t, came[t][which].astype(F32), part)
                    parts.append(decoded(part[:, :rows], bound_at(part, rows)))
                return jnp.concatenate(parts, axis=1) if ratio > 1 else parts[0]

            same = same[...]
            square = same[:, :cols]
            other = mirrored(1)
            a = index[4] * rows + iota(square.shape, 0)
            b = index[5] * cols + iota(square.shape, 1)
            out00 = jnp.where(a <= b, square, other)
            out11 = jnp.where(a > b, square, jnp.where(a == b, same[:, cols : cols + 1], other))
            return [out00, crossed[...][:, :cols], mirrored(0), out11]

        def outcome_kernel(index, *refs):
            for n, block in enumerate(outcome(index, *refs[:-1])):
                refs[-1][n // 2, :, n % 2, :] = block

        def kind(shape, dtype=F32):
            return jax.ShapeDtypeStruct(shape, dtype)

        work = amplitudes.size * virtuals

        def across_core(pair_of):
            return pair_of[0], send(pair_of[1], lambda p, v: (p, v ^ 1))

        def across_plane(index, kept, came):
            shape = (nx, nz, 2, rows, width)
            types = [kind((nz, rows, width))] + [kind((nz, rows, width), BF16)] * len(steps)
            own, *outs = local(chip_sum, types, aligned, "chip_sum", work)(index, kept.reshape(shape), came.reshape(shape))
            came = [send(block, lambda p, v: (p ^ dy, (v + 2 * dx) % nv)) for (dx, dy), block in zip(steps, outs)]
            return own, came

        def across_line(index, own, came):
            types = [kind((rows, width))] + [kind((rows, width), BF16)] * (nz - 1)
            own, *outs = local(plane_sum, types, aligned, "plane_sum", 2 * work)(index, own, *came)
            return own, [send(block, lambda p, v: (p ^ 2 * dz, v)) for dz, block in zip(range(1, nz), outs)]

        def line_total(index, own, came, first_tiles=()):
            shape = (2, rows, tile_width) if first_tiles else (rows, tile_width)
            types = [kind((rows, width))] + [kind(shape, BF16)] * ratio
            body = line_sum(len(came), bool(first_tiles))
            return local(body, types, aligned, "line_sum")(index, own, *came, *first_tiles)

        def exchanged(tiles):
            return [
                send(tile, lambda p, v: (ratio * v + (p % ratio + t) % ratio, p // ratio)) for t, tile in enumerate(tiles)
            ]

        if aligned:
            half_types = [kind((nx, virtuals, width))] * 2
            crossed, u, w = crossed_sums(index, amplitudes, integrals, half_types, cols)
            crossed = across_core(crossed)
            square = kind((virtuals // 2, virtuals))
            (p00,), u, w = on_chip(
                first_square_kernel, "first_square", [square], [], work // 2, after(index, crossed[0]), u, w
            )
            crossed = across_plane(after(index, p00), *crossed)
            placed = kind((nv, virtuals, width))
            (p00_rest, p11, out, largest), u, w = on_chip(
                other_squares_kernel(cols),
                "other_squares",
                [square, kind((virtuals, virtuals)), placed, kind((1, cols))],
                [],
                3 * work // 2,
                after(index, crossed[0]),
                u,
                w,
                p00,
            )
            *same, _ = pl.pallas_call(
                same_kernel(cols),
                in_specs=[SMEM] + [VMEM] * 5,
                out_specs=[VMEM] * 3,
                out_shape=[*half_types, placed],
                input_output_aliases={1: 2},
                name="same",
                cost_estimate=pl.CostEstimate(flops=work // 2, bytes_accessed=2**20, transcendentals=0),
                compiler_params=pltpu.CompilerParams(vmem_limit_bytes=3 * 2**20),
            )(after(index, p11, *crossed[1]), out, p00, p00_rest, p11, largest)
            crossed = across_line(after(index, same[0]), *crossed)
            same = across_core(same)
            same = across_plane(after(index, crossed[0]), *same)
            crossed, *tiles = line_total(after(index, same[0]), *crossed)
            same = across_line(after(index, crossed), *same)
        else:
            crossed, same = (
                across_line(index, *across_plane(index, *across_core(plain_sums(index, amplitudes, integrals, kind_same, nv, width))))
                for kind_same in (False, True)
            )
            crossed, *tiles = line_total(index, *crossed)
        same, *tiles = line_total(index, *same, tiles)
        arrays = [crossed, same, *exchanged(tiles)]
        if not aligned:
            blocks = outcome(index, *arrays)
            return jnp.stack([jnp.stack(blocks[:2], 1), jnp.stack(blocks[2:], 1)])
        return pl.pallas_call(
            outcome_kernel,
            in_specs=[SMEM] + [VMEM] * len(arrays),
            out_specs=VMEM,
            out_shape=kind((2, rows, 2, cols)),
            name="outcome",
            compiler_params=pltpu.CompilerParams(vmem_limit_bytes=8 * 2**20),
        )(index, *arrays)

    placed = (P(None, "pair", None, "virt"), P("pair", "virt", None, None))
    return jax.shard_map(
        shards, mesh=mesh, in_specs=placed, out_specs=P(None, "pair", None, "virt"), check_vma=False
    )
```
